1024 devices in a mesh: group: 16 (over y, z_hi), inner: 64 (over x, z_lo, core).
Axes of the slice: x: 4, y: 4, z: 32 (z_hi: 4, z_lo: 8; z = z_hi * 8 + z_lo), core: 2. Of those that a mesh axis runs over, the one named last changes fastest.
Arguments:
- tokens: bfloat16 [196608, 8192], P(('group', 'inner')), may hold values from -24 to 24
- weight_codes: bfloat16 [8192, 128], P('inner'), may hold values from -4 to 4
- weight_exp: int32 [64], replicated, may hold values from -9 to -5
- grad_exp: int32 [64], replicated, may hold values from -15 to -9
- recast_exp: int32 [64], replicated, may hold values from 0 to 5
- out_grad: bfloat16 [196608, 128], P(('group', 'inner')), may hold values from -0.0234375 to 0.0234375
Outputs:
- activation: bfloat16 [196608, 128], P(('group', 'inner'))
- grad_sum: float32 [8192, 128], P(('inner', 'group'))
The draws below stay inside these ranges and needn't reach their ends.
All inputs are finite; a program needn't handle non-finite values.
Results may differ from the reference program's by a relative error of at most 0.0085.
Values may be sent and summed in bfloat16 or wider, within the bound.
A program may use at most 32 MiB of HBM per device.

```python
import jax
import jax.numpy as jnp
from jax import lax

D = 8192
QB = 128
TOK_DEV = 192
TOKENS = 196608
N_GROUP = 16
N_INNER = 64


def touch_ends(result, stream_key, least, high):
    extent = result.shape
    index_at = [jax.random.randint(jax.random.fold_in(stream_key, axis), (), 0, extent[axis]) for axis in range(len(extent))]
    result = result.at[tuple(index_at)].set(least)
    longest = extent.index(max(extent))
    index_at[longest] = (index_at[longest] + 1) % extent[longest]
    return result.at[tuple(index_at)].set(high)


def strengthened(array, stream_key, source, target, blocks, factor):
    owner, partner = [(jnp.arange(array.shape[axis_at]) // (array.shape[axis_at] // blocks)).reshape([-1 if axis == axis_at else 1 for axis in range(array.ndim)]) for axis_at in (source, target)]
    chosen = jax.random.permutation(stream_key, blocks)[partner]
    strong = (owner == chosen) | (owner == (partner + blocks // 2) % blocks)
    return jnp.where(strong, factor * array, array)


def block_levels(own_key, extent, pieces, smallest, top_value):
    def one(axis_at, shards_of):
        steps = jax.random.uniform(jax.random.fold_in(jax.random.fold_in(own_key, 6), axis_at), (shards_of,), jnp.float32, smallest / len(pieces), top_value / len(pieces))
        return jnp.repeat(jnp.exp(steps), extent[axis_at] // shards_of).reshape((-1,) + (1,) * (len(extent) - axis_at - 1))

    loudness = one(*pieces[0])
    for cut in pieces[1:]:
        loudness = loudness * one(*cut)
    return loudness


def centred(own_key, shape, deviation, most, split=(), dtype=jnp.bfloat16):
    loudness = block_levels(own_key, shape, split, -0.22, 0.18) if split else 1.0
    array = jax.random.normal(own_key, shape, jnp.float32) * deviation * loudness
    return jnp.minimum(jnp.maximum(array, -most), most).astype(dtype)


def gaussian_with(stream_key, shape, deviation, reach, shards, heavy, kind=jnp.bfloat16):
    drawn = deviation * jax.random.normal(stream_key, shape, jnp.float32)
    if shards:
        drawn = drawn * block_levels(stream_key, shape, shards, -0.22, 0.18)
    return jnp.clip(strengthened(drawn, jax.random.fold_in(stream_key, 3), *heavy), -reach, reach).astype(kind)


def setup_inputs(seed: int = 0) -> dict:
    seeds = jax.random.split(jax.random.key(seed), 7)
    tokens = gaussian_with(seeds[0], (TOKENS, D), 1.0, 24.0, ((0, 1024),), (0, 1, 1024, 6.0))
    weight_codes = centred(seeds[1], (D, QB), 1.0, 4.0, ((0, 64),))
    weight_exp = touch_ends(jax.random.randint(seeds[2], (D // QB,), -9, -4), jax.random.fold_in(seeds[2], 1), -9, (-4) - 1).astype(jnp.int32)
    grad_exp = touch_ends(jax.random.randint(seeds[3], (D // QB,), -15, -8), jax.random.fold_in(seeds[3], 1), -15, (-8) - 1).astype(jnp.int32)
    recast_exp = touch_ends(jax.random.randint(seeds[4], (D // QB,), 0, 6), jax.random.fold_in(seeds[4], 1), 0, 5).astype(jnp.int32)
    out_grad = centred(seeds[5], (TOKENS, QB), 0.00390625, 0.0234375, ((0, 1024),))
    return dict(tokens=tokens, weight_codes=weight_codes, weight_exp=weight_exp, grad_exp=grad_exp, recast_exp=recast_exp, out_grad=out_grad)


code_limit = 448.0


def row_scale(exponents, sign):
    rows = jnp.repeat(exponents, QB).astype(jnp.float32)
    return jnp.exp2(sign * rows)[:, None]


def reference(tokens, weight_codes, weight_exp, grad_exp, recast_exp, out_grad):
    weight = (weight_codes.astype(jnp.float32) * row_scale(weight_exp, 1.0)).astype(jnp.bfloat16)
    inv_grad = row_scale(grad_exp, -1.0)
    inv_recast = row_scale(recast_exp, -1.0)
    scale_back = row_scale(grad_exp + recast_exp, 1.0)
    token_blocks = tokens.reshape(N_GROUP, N_INNER, TOK_DEV, D)
    grad_blocks = out_grad.reshape(N_GROUP, N_INNER, TOK_DEV, QB)

    def device_step(pair):
        inputs, cotangent = pair
        pre = jnp.dot(inputs, weight, preferred_element_type=jnp.float32)
        sig = jax.nn.sigmoid(pre)
        activation = (pre * sig).astype(jnp.bfloat16)
        delta = (cotangent.astype(jnp.float32) * sig * (1.0 + pre * (1.0 - sig))).astype(jnp.bfloat16)
        partial_grad = lax.dot_general(inputs, delta, (((0,), (0,)), ((), ())), preferred_element_type=jnp.float32)
        coded = jnp.clip(partial_grad * inv_grad, -code_limit, code_limit).astype(jnp.bfloat16)
        return activation, coded

    def group_step(pair):
        activations, coded = lax.map(device_step, pair)
        first = jnp.sum(coded.astype(jnp.float32), axis=0)
        recoded = jnp.clip(first * inv_recast, -code_limit, code_limit).astype(jnp.bfloat16)
        return activations, recoded

    activations, recoded = lax.map(group_step, (token_blocks, grad_blocks))
    grad_sum = jnp.sum(recoded.astype(jnp.float32), axis=0) * scale_back
    return activations.reshape(TOKENS, QB), grad_sum
```

```python
import jax
import jax.numpy as jnp
from jax import lax
from jax.experimental import pallas as pl
from jax.experimental.pallas import tpu as pltpu
from jax.sharding import PartitionSpec as P

code_limit = 448.0
MESH = pl.DeviceIdType.MESH
NX, NY, NZ, RUN = 4, 4, 32, 8
QB, TOK = 128, 192


def mod(a, n):
    return lax.rem(a + 2 * n, n)


def coords():
    g = lax.axis_index("group")
    i = lax.axis_index("inner")
    return i // 16, g // 4, (g % 4) * RUN + (i // 2) % RUN, i % 2


def dev(x, y, z, c):
    x, y, z = mod(x, NX), mod(y, NY), mod(z, NZ)
    return (y * (NZ // RUN) + z // RUN, (x * RUN + z % RUN) * 2 + c)


def pow2(e):
    return jnp.left_shift(jnp.int32(1), e + 15).astype(jnp.float32) * (2.0**-15)


def block(x, zl, c):
    return (x * RUN + zl) * 2 + c


def kernel(
    tok_hbm, codes_hbm, wexp_hbm, gexp_hbm, rexp_hbm, og_hbm,
    act_out, grad_out,
    tok, codes, og, wexp, gexp, rexp,
    wbuf, act, dt, cod, sibin, xout, xin, zout, zin, pout, pin,
    load_sem, act_sem,
    gz_s, gz_r, gx_s, gx_r, gc_s, gc_r,
    sib_s, sib_r, rx_s, rx_r, rz_s, rz_r, p_s, p_r,
    know1, know2,
):
    x, y, z, c = coords()
    zl = z % RUN
    run0 = z - zl
    even = (x + c) % 2 == 0
    four = jnp.where(even, 4, -4)

    loads = [
        pltpu.make_async_copy(src, dst, load_sem.at[k])
        for k, (src, dst) in enumerate(
            ((codes_hbm, codes), (wexp_hbm, wexp), (gexp_hbm, gexp), (rexp_hbm, rexp), (og_hbm, og), (tok_hbm, tok))
        )
    ]
    for copy in loads:
        copy.start()

    barrier = pltpu.get_barrier_semaphore()
    near = [dev(x, y, z, 1 - c)]
    near += [dev(x + d, y, z, c) for d in (1, 2, 3)]
    near += [dev(x, y + d, z, c) for d in (1, 2, 3)]
    near += [dev(x, y, z + d, c) for d in (1, -1, 2, -2, 3, -3, 4, -4)]
    for who in near:
        pl.semaphore_signal(barrier, inc=1, device_id=who, device_id_type=MESH)

    loads[0].wait()
    loads[1].wait()
    own = codes[...].astype(jnp.float32) * pow2(wexp[block(x, zl, c)])
    wbuf[zl, x, c] = own.astype(jnp.bfloat16)
    pl.semaphore_wait(barrier, len(near))

    def offset(k):
        return jnp.where(k == 6, four, (k // 2 + 1) * (1 - 2 * (k % 2)))

    def origin(k):
        return jnp.where(k == 7, zl, mod(zl - offset(k), RUN))

    def gz(k):
        slot = wbuf.at[zl, x, c]
        return pltpu.make_async_remote_copy(
            src_ref=slot, dst_ref=slot, send_sem=gz_s.at[k], recv_sem=gz_r.at[k],
            device_id=dev(x, y, z + offset(k), c), device_id_type=MESH,
        )

    def gz_wait(k):
        slot = wbuf.at[origin(k), x, c]
        pltpu.make_async_remote_copy(
            src_ref=slot, dst_ref=slot, send_sem=gz_s.at[k], recv_sem=gz_r.at[k],
            device_id=dev(x, y, z + offset(k), c), device_id_type=MESH,
        ).wait_recv()

    def gx(k, d, shift):
        slot = wbuf.at[origin(k), mod(x + shift, NX), c]
        return pltpu.make_async_remote_copy(
            src_ref=slot, dst_ref=slot, send_sem=gx_s.at[k, d - 1], recv_sem=gx_r.at[k, d - 1],
            device_id=dev(x + d, y, z, c), device_id_type=MESH,
        )

    def gc(zs, xs, cs):
        slot = wbuf.at[zs, xs, cs]
        return pltpu.make_async_remote_copy(
            src_ref=slot, dst_ref=slot, send_sem=gc_s.at[zs, xs], recv_sem=gc_r.at[zs, xs],
            device_id=dev(x, y, z, 1 - c), device_id_type=MESH,
        )

    def each(n, f):
        lax.fori_loop(0, n, lambda k, _: (f(k), 0)[1], 0)

    each(7, lambda k: gz(6 - k).start())

    def pass_on(k):
        for d in (2, 1, 3):
            gx(k, d, 0).start()
        gc(origin(k), x, c).start()

    pass_on(jnp.int32(7))

    def arrived_z(k):
        gz_wait(k)
        pass_on(k)

    each(7, arrived_z)

    def arrived_x(k):
        k = lax.rem(k + 7, 8)
        for d in (1, 3, 2):
            gx(k, d, -d).wait_recv()
            gc(origin(k), mod(x - d, NX), c).start()

    each(8, arrived_x)

    for copy in loads[2:]:
        copy.wait()

    for d in (4, -4):
        pl.semaphore_signal(know1, inc=1, device_id=dev(x, y, z + d, c), device_id_type=MESH)

    def arrived_c(k):
        gc(k // NX, k % NX, 1 - c).wait_recv()

    each(32, arrived_c)

    def product(k, acc):
        for xs in range(NX):
            cols = pl.ds(pl.multiple_of((xs * RUN + k) * 256, 256), 256)
            w = wbuf[k, xs].reshape(2 * QB, QB)
            acc += jnp.dot(tok[:, cols], w, preferred_element_type=jnp.float32)
        return acc

    pre = lax.fori_loop(0, RUN, product, jnp.zeros((TOK, QB), jnp.float32))
    sig = jax.nn.sigmoid(pre)
    act[...] = (pre * sig).astype(jnp.bfloat16)
    act_copy = pltpu.make_async_copy(act, act_out, act_sem)
    act_copy.start()
    delta = og[...].astype(jnp.float32) * sig * (1.0 + pre * (1.0 - sig))
    dt[...] = delta.astype(jnp.bfloat16).T

    def place(k):
        return mod(zl + k + 1, RUN)

    def sib(k, side):
        return pltpu.make_async_remote_copy(
            src_ref=cod.at[k, side], dst_ref=sibin.at[k], send_sem=sib_s.at[k], recv_sem=sib_r.at[k],
            device_id=dev(x, y, z, 1 - c), device_id_type=MESH,
        )

    def rx(k, d):
        return pltpu.make_async_remote_copy(
            src_ref=xout.at[k, mod(x + d, NX)], dst_ref=xin.at[k, d - 1], send_sem=rx_s.at[k, d - 1],
            recv_sem=rx_r.at[k, d - 1], device_id=dev(x + d, y, z, c), device_id_type=MESH,
        )

    def rz(k):
        return pltpu.make_async_remote_copy(
            src_ref=zout.at[k], dst_ref=zin.at[k], send_sem=rz_s.at[k], recv_sem=rz_r.at[k],
            device_id=dev(x, y, run0 + place(k), c), device_id_type=MESH,
        )

    def coded(k):
        zs = mod(place(k) + 4, RUN)
        for xs in range(NX):
            cols = pl.ds(pl.multiple_of((xs * RUN + zs) * 256, 256), 256)
            part = jnp.dot(dt[...], tok[:, cols], preferred_element_type=jnp.float32)
            for cs in range(2):
                scaled = part[:, cs * QB:(cs + 1) * QB] * pow2(-gexp[block(xs, zs, cs)])
                cod[k, cs, xs] = jnp.clip(scaled, -code_limit, code_limit).astype(jnp.bfloat16)
        sib(k, 1 - c).start()

    def over_cores(k):
        sib(k, 1 - c).wait_recv()
        for xs in range(NX):
            both = cod[k, c, xs].astype(jnp.float32) + sibin[k, xs].astype(jnp.float32)
            xout[k, xs] = both.astype(jnp.bfloat16)
        for d in (2, 1, 3):
            rx(k, d).start()

    def over_x(k):
        total = xout[k, x].astype(jnp.float32)
        for d in (1, 3, 2):
            rx(k, d).wait_recv()
            total += xin[k, d - 1].astype(jnp.float32)
        zout[k] = total.astype(jnp.bfloat16)

        @pl.when(k < 7)
        def _():
            rz(k).start()

    def stage(k):
        @pl.when(k < 8)
        def _():
            coded(k)

        @pl.when((k >= 1) & (k < 9))
        def _():
            over_cores(k - 1)

        @pl.when(k >= 2)
        def _():
            over_x(k - 2)

    each(10, stage)

    pl.semaphore_wait(know1, 2)
    for d in (8, -8):
        pl.semaphore_signal(know2, inc=1, device_id=dev(x, y, z + d, c), device_id_type=MESH)

    def add_z(k, acc):
        rz(k).wait_recv()
        return acc + zin[k].astype(jnp.float32)

    first = lax.fori_loop(0, 7, add_z, zout[7].astype(jnp.float32))
    zl4 = mod(zl + 4, RUN)
    recoded = jnp.clip(first * pow2(-rexp[block(x, zl4, c)]), -code_limit, code_limit)
    recoded = recoded.astype(jnp.bfloat16).astype(jnp.float32)
    pout[...] = recoded.T.reshape(16, 8, QB)
    pl.semaphore_wait(know2, 2)

    me = lax.axis_index("group")

    def piece(k):
        there = mod(me + k, 16)
        return pltpu.make_async_remote_copy(
            src_ref=pout.at[there], dst_ref=pin.at[k], send_sem=p_s.at[k], recv_sem=p_r.at[k],
            device_id=(there, block(x, zl4, c)), device_id_type=MESH,
        )

    each(16, lambda k: piece(k).start())

    def add_piece(k, acc):
        piece(k).wait_recv()
        return acc + pin[k]

    summed = lax.fori_loop(0, 16, add_piece, jnp.zeros((8, QB), jnp.float32))
    mine = block(x, zl, c)
    grad_out[...] = summed * pow2(gexp[mine] + rexp[mine])

    each(7, lambda k: gz(k).wait_send())

    def sent8(k):
        for d in (1, 2, 3):
            gx(k, d, 0).wait_send()
            rx(k, d).wait_send()
        sib(k, 1 - c).wait_send()

    each(8, sent8)
    each(32, lambda k: gc(k // NX, k % NX, c).wait_send())
    each(7, lambda k: rz(k).wait_send())
    each(16, lambda k: piece(k).wait_send())
    act_copy.wait()


def body(tokens, weight_codes, weight_exp, grad_exp, recast_exp, out_grad):
    bf, f32 = jnp.bfloat16, jnp.float32
    dma, vmem = pltpu.SemaphoreType.DMA, pltpu.VMEM
    return pl.pallas_call(
        kernel,
        name="mlp_block",
        out_shape=(jax.ShapeDtypeStruct((TOK, QB), bf), jax.ShapeDtypeStruct((8, QB), f32)),
        in_specs=[pl.BlockSpec(memory_space=pl.ANY)] * 6,
        out_specs=(pl.BlockSpec(memory_space=pl.ANY), pl.BlockSpec(memory_space=pltpu.VMEM)),
        scratch_shapes=[
            vmem((TOK, 8192), bf), vmem((QB, QB), bf), vmem((TOK, QB), bf),
            pltpu.SMEM((64,), jnp.int32), pltpu.SMEM((64,), jnp.int32), pltpu.SMEM((64,), jnp.int32),
            vmem((RUN, NX, 2, QB, QB), bf), vmem((TOK, QB), bf), vmem((QB, TOK), bf),
            vmem((RUN, 2, NX, QB, QB), bf), vmem((RUN, NX, QB, QB), bf),
            vmem((RUN, NX, QB, QB), bf), vmem((RUN, 3, QB, QB), bf),
            vmem((RUN, QB, QB), bf), vmem((7, QB, QB), bf),
            vmem((16, 8, QB), f32), vmem((16, 8, QB), f32),
            dma((6,)), dma,
            dma((7,)), dma((7,)), dma((8, 3)), dma((8, 3)), dma((8, 4)), dma((8, 4)),
            dma((8,)), dma((8,)), dma((8, 3)), dma((8, 3)), dma((7,)), dma((7,)), dma((16,)), dma((16,)),
            pltpu.SemaphoreType.REGULAR, pltpu.SemaphoreType.REGULAR,
        ],
        compiler_params=pltpu.CompilerParams(
            collective_id=0, has_side_effects=True, vmem_limit_bytes=40 * 2**20
        ),
    )(tokens, weight_codes, weight_exp, grad_exp, recast_exp, out_grad)


def solution(mesh):
    placed = (
        P(("group", "inner"), None),
        P("inner", None),
        P(),
        P(),
        P(),
        P(("group", "inner"), None),
    )
    return jax.shard_map(
        body,
        mesh=mesh,
        in_specs=placed,
        out_specs=(P(("group", "inner"), None), P(("inner", "group"), None)),
        check_vma=False,
    )
```

```python
import jax
import jax.numpy as jnp
from jax import lax
from jax.experimental import pallas as pl
from jax.experimental.pallas import tpu as pltpu
from jax.sharding import PartitionSpec as P

code_limit = 448.0
MESH = pl.DeviceIdType.MESH
NX, NY, NZ, RUN = 4, 4, 32, 8
QB, TOK = 128, 192


def mod(a, n):
    return lax.rem(a + 2 * n, n)


def coords():
    g = lax.axis_index("group")
    i = lax.axis_index("inner")
    return i // 16, g // 4, (g % 4) * RUN + (i // 2) % RUN, i % 2


def dev(x, y, z, c):
    x, y, z = mod(x, NX), mod(y, NY), mod(z, NZ)
    return (y * (NZ // RUN) + z // RUN, (x * RUN + z % RUN) * 2 + c)


def pow2(e):
    return jnp.left_shift(jnp.int32(1), e + 15).astype(jnp.float32) * (2.0**-15)


def block(x, zl, c):
    return (x * RUN + zl) * 2 + c


def kernel(
    tok_hbm, codes_hbm, wexp_hbm, gexp_hbm, rexp_hbm, og_hbm,
    act_out, grad_out,
    tok, codes, og, wexp, gexp, rexp,
    wbuf, act, dt, cod, sibin, xout, xin, zout, zin, pout, pin,
    load_sem, act_sem,
    gz_s, gz_r, gx_s, gx_r, gy_s, gy_r, gc_s, gc_r,
    sib_s, sib_r, rx_s, rx_r, rz_s, rz_r, p_s, p_r,
    know1, know2,
):
    x, y, z, c = coords()
    zl = z % RUN
    run0 = z - zl

    loads = [
        pltpu.make_async_copy(src, dst, load_sem.at[k])
        for k, (src, dst) in enumerate(
            ((codes_hbm, codes), (wexp_hbm, wexp), (gexp_hbm, gexp), (rexp_hbm, rexp), (og_hbm, og), (tok_hbm, tok))
        )
    ]
    for copy in loads:
        copy.start()

    barrier = pltpu.get_barrier_semaphore()
    near = [dev(x, y, z, 1 - c)]
    near += [dev(x + d, y, z, c) for d in (1, 2, 3)]
    near += [dev(x, y + d, z, c) for d in (1, 3)]
    near += [dev(x, y, z + d, c) for d in (1, -1, 2, -2, 3, -3, 4, -4)]
    for who in near:
        pl.semaphore_signal(barrier, inc=1, device_id=who, device_id_type=MESH)

    loads[0].wait()
    loads[1].wait()
    own = codes[...].astype(jnp.float32) * pow2(wexp[block(x, zl, c)])
    wbuf[zl, x, c] = own.astype(jnp.bfloat16)
    pl.semaphore_wait(barrier, len(near))

    odd = (zl + y) % 2
    four = jnp.where((x + c) % 2 == 0, 4, -4)

    def origin(k, odd):
        straight = jnp.where(k == 3, 4, jnp.where(k == 2, -2, 2 * k))
        crossed = (k // 2 * 2 + 1) * (1 - 2 * (k % 2))
        return mod(zl + jnp.where(odd == 1, crossed, straight), RUN)

    def gz(n, far, k):
        slot = wbuf.at[zl, x, c]
        return pltpu.make_async_remote_copy(
            src_ref=slot, dst_ref=slot, send_sem=gz_s.at[n], recv_sem=gz_r.at[k],
            device_id=dev(x, y, z + far, c), device_id_type=MESH,
        )

    def gz_wait(k):
        slot = wbuf.at[origin(k, odd), x, c]
        pltpu.make_async_remote_copy(
            src_ref=slot, dst_ref=slot, send_sem=gz_s.at[k], recv_sem=gz_r.at[k],
            device_id=dev(x, y, z + 1, c), device_id_type=MESH,
        ).wait_recv()

    def gx(k, d, shift):
        slot = wbuf.at[origin(k, odd), mod(x + shift, NX), c]
        return pltpu.make_async_remote_copy(
            src_ref=slot, dst_ref=slot, send_sem=gx_s.at[k, d - 1], recv_sem=gx_r.at[k, d - 1],
            device_id=dev(x + d, y, z, c), device_id_type=MESH,
        )

    def gy(k, xs, odd):
        slot = wbuf.at[origin(k, odd), xs, c]
        return pltpu.make_async_remote_copy(
            src_ref=slot, dst_ref=slot, send_sem=gy_s.at[k, xs], recv_sem=gy_r.at[k, xs],
            device_id=dev(x, y + 1 - 2 * (xs % 2), z, c), device_id_type=MESH,
        )

    def gc(zs, xs, cs):
        slot = wbuf.at[zs, xs, cs]
        return pltpu.make_async_remote_copy(
            src_ref=slot, dst_ref=slot, send_sem=gc_s.at[zs, xs], recv_sem=gc_r.at[zs, xs],
            device_id=dev(x, y, z, 1 - c), device_id_type=MESH,
        )

    def each(n, f):
        lax.fori_loop(0, n, lambda k, _: (f(k), 0)[1], 0)

    from_own = [gz(n, far, k) for n, (far, k) in enumerate(
        ((1, 1), (-1, 0), (3, 3), (-3, 2), (four, 3), (2, 2), (-2, 1))
    )]

    @pl.when(odd == 0)
    def _():
        for copy in from_own:
            copy.start()

    @pl.when(odd == 1)
    def _():
        gc(zl, x, c).start()

    def arrived_z(k):
        @pl.when((odd == 1) | (k > 0))
        def _():
            gz_wait(k)

        for d in (2, 1, 3):
            gx(k, d, 0).start()

        @pl.when((odd == 1) | (k > 0))
        def _():
            gy(k, x, odd).start()

        gc(origin(k, odd), x, c).start()

    def arrived_x(k):
        for d in (1, 3, 2):
            gx(k, d, -d).wait_recv()
            gy(k, mod(x - d, NX), odd).start()
            gc(origin(k, odd), mod(x - d, NX), c).start()

    def gather(k):
        @pl.when(k >= 3)
        def _():
            arrived_x(k - 3)

        @pl.when(k < 4)
        def _():
            arrived_z(k)

    each(7, gather)

    def arrived_y(k):
        for xs in range(NX):
            @pl.when((odd == 0) | (k > 0) | (xs != x))
            def _():
                gy(k, xs, 1 - odd).wait_recv()
                gc(origin(k, 1 - odd), xs, c).start()

    each(4, arrived_y)

    for copy in loads[2:]:
        copy.wait()

    for d in (4, -4):
        pl.semaphore_signal(know1, inc=1, device_id=dev(x, y, z + d, c), device_id_type=MESH)

    def arrived_c(k):
        gc(k // NX, k % NX, 1 - c).wait_recv()

    each(32, arrived_c)

    def product(k, acc):
        for xs in range(NX):
            cols = pl.ds(pl.multiple_of((xs * RUN + k) * 256, 256), 256)
            w = wbuf[k, xs].reshape(2 * QB, QB)
            acc += jnp.dot(tok[:, cols], w, preferred_element_type=jnp.float32)
        return acc

    pre = lax.fori_loop(0, RUN, product, jnp.zeros((TOK, QB), jnp.float32))
    sig = jax.nn.sigmoid(pre)
    act[...] = (pre * sig).astype(jnp.bfloat16)
    act_copy = pltpu.make_async_copy(act, act_out, act_sem)
    act_copy.start()
    delta = og[...].astype(jnp.float32) * sig * (1.0 + pre * (1.0 - sig))
    dt[...] = delta.astype(jnp.bfloat16).T

    up = zl * 2 < RUN
    short, long = jnp.where(up, zl, 7 - zl), jnp.where(up, 7 - zl, zl)

    def place(k):
        both = k - (long - short)
        far = jnp.where(both < 0, long - k, short - both // 2)
        ahead = up ^ ((both >= 0) & (both % 2 == 1))
        return zl + jnp.where(ahead, far, -far)

    def sib(k, side):
        return pltpu.make_async_remote_copy(
            src_ref=cod.at[k, side], dst_ref=sibin.at[k], send_sem=sib_s.at[k], recv_sem=sib_r.at[k],
            device_id=dev(x, y, z, 1 - c), device_id_type=MESH,
        )

    def rx(k, d):
        return pltpu.make_async_remote_copy(
            src_ref=xout.at[k, mod(x + d, NX)], dst_ref=xin.at[k, d - 1], send_sem=rx_s.at[k, d - 1],
            recv_sem=rx_r.at[k, d - 1], device_id=dev(x + d, y, z, c), device_id_type=MESH,
        )

    def rz(k):
        return pltpu.make_async_remote_copy(
            src_ref=zout.at[k], dst_ref=zin.at[zl], send_sem=rz_s.at[k], recv_sem=rz_r.at[zl],
            device_id=dev(x, y, run0 + place(k), c), device_id_type=MESH,
        )

    def rz_wait(k):
        there = place(k)
        pltpu.make_async_remote_copy(
            src_ref=zout.at[k], dst_ref=zin.at[there], send_sem=rz_s.at[k], recv_sem=rz_r.at[there],
            device_id=dev(x, y, run0 + there, c), device_id_type=MESH,
        ).wait_recv()

    def coded(k):
        zs = mod(place(k) + 4, RUN)
        for xs in range(NX):
            cols = pl.ds(pl.multiple_of((xs * RUN + zs) * 256, 256), 256)
            part = jnp.dot(dt[...], tok[:, cols], preferred_element_type=jnp.float32)
            for cs in range(2):
                scaled = part[:, cs * QB:(cs + 1) * QB] * pow2(-gexp[block(xs, zs, cs)])
                cod[k, cs, xs] = jnp.clip(scaled, -code_limit, code_limit).astype(jnp.bfloat16)
        sib(k, 1 - c).start()

    def over_cores(k):
        sib(k, 1 - c).wait_recv()
        for xs in range(NX):
            both = cod[k, c, xs].astype(jnp.float32) + sibin[k, xs].astype(jnp.float32)
            xout[k, xs] = both.astype(jnp.bfloat16)
        for d in (2, 1, 3):
            rx(k, d).start()

    def over_x(k):
        total = xout[k, x].astype(jnp.float32)
        for d in (1, 3, 2):
            rx(k, d).wait_recv()
            total += xin[k, d - 1].astype(jnp.float32)
        zout[k] = total.astype(jnp.bfloat16)

        @pl.when(k < 7)
        def _():
            rz(k).start()

    def stage(k):
        @pl.when(k < 8)
        def _():
            coded(k)

        @pl.when((k >= 1) & (k < 9))
        def _():
            over_cores(k - 1)

        @pl.when(k == 2)
        def _():
            pl.semaphore_wait(know1, 2)
            for d in (8, -8):
                pl.semaphore_signal(know2, inc=1, device_id=dev(x, y, z + d, c), device_id_type=MESH)

        @pl.when(k >= 2)
        def _():
            over_x(k - 2)

    each(10, stage)

    def add_z(k, acc):
        rz_wait(k)
        return acc + zin[place(k)].astype(jnp.float32)

    first = lax.fori_loop(0, 7, add_z, zout[7].astype(jnp.float32))
    zl4 = mod(zl + 4, RUN)
    recoded = jnp.clip(first * pow2(-rexp[block(x, zl4, c)]), -code_limit, code_limit)
    recoded = recoded.astype(jnp.bfloat16).astype(jnp.float32)
    pout[...] = recoded.T.reshape(16, 8, QB)
    pl.semaphore_wait(know2, 2)

    me = lax.axis_index("group")

    def piece(k):
        there = mod(me + k, 16)
        return pltpu.make_async_remote_copy(
            src_ref=pout.at[there], dst_ref=pin.at[k], send_sem=p_s.at[k], recv_sem=p_r.at[k],
            device_id=(there, block(x, zl4, c)), device_id_type=MESH,
        )

    each(16, lambda k: piece(k).start())

    def add_piece(k, acc):
        piece(k).wait_recv()
        return acc + pin[k]

    summed = lax.fori_loop(0, 16, add_piece, jnp.zeros((8, QB), jnp.float32))
    mine = block(x, zl, c)
    grad_out[...] = summed * pow2(gexp[mine] + rexp[mine])

    @pl.when(odd == 0)
    def _():
        for copy in from_own:
            copy.wait_send()

    def sent4(k):
        for d in (1, 2, 3):
            gx(k, d, 0).wait_send()
        for xs in range(NX):
            @pl.when((odd == 1) | (k > 0) | (xs != x))
            def _():
                gy(k, xs, odd).wait_send()

    each(4, sent4)
    each(32, lambda k: gc(k // NX, k % NX, c).wait_send())
    act_copy.wait()

    def sent8(k):
        for d in (1, 2, 3):
            rx(k, d).wait_send()
        sib(k, 1 - c).wait_send()

    each(8, sent8)
    each(7, lambda k: rz(k).wait_send())
    each(16, lambda k: piece(k).wait_send())


def body(tokens, weight_codes, weight_exp, grad_exp, recast_exp, out_grad):
    bf, f32 = jnp.bfloat16, jnp.float32
    dma, vmem = pltpu.SemaphoreType.DMA, pltpu.VMEM
    return pl.pallas_call(
        kernel,
        name="mlp_block",
        out_shape=(jax.ShapeDtypeStruct((TOK, QB), bf), jax.ShapeDtypeStruct((8, QB), f32)),
        in_specs=[pl.BlockSpec(memory_space=pltpu.HBM)] * 6,
        out_specs=(pl.BlockSpec(memory_space=pltpu.HBM), pl.BlockSpec(memory_space=pltpu.VMEM)),
        scratch_shapes=[
            vmem((TOK, 8192), bf), vmem((QB, QB), bf), vmem((TOK, QB), bf),
            pltpu.SMEM((64,), jnp.int32), pltpu.SMEM((64,), jnp.int32), pltpu.SMEM((64,), jnp.int32),
            vmem((RUN, NX, 2, QB, QB), bf), vmem((TOK, QB), bf), vmem((QB, TOK), bf),
            vmem((RUN, 2, NX, QB, QB), bf), vmem((RUN, NX, QB, QB), bf),
            vmem((RUN, NX, QB, QB), bf), vmem((RUN, 3, QB, QB), bf),
            vmem((RUN, QB, QB), bf), vmem((RUN, QB, QB), bf),
            vmem((16, 8, QB), f32), vmem((16, 8, QB), f32),
            dma((6,)), dma,
            dma((7,)), dma((4,)), dma((4, 3)), dma((4, 3)), dma((4, 4)), dma((4, 4)), dma((8, 4)), dma((8, 4)),
            dma((8,)), dma((8,)), dma((8, 3)), dma((8, 3)), dma((7,)), dma((8,)), dma((16,)), dma((16,)),
            pltpu.SemaphoreType.REGULAR, pltpu.SemaphoreType.REGULAR,
        ],
        compiler_params=pltpu.CompilerParams(
            collective_id=0, has_side_effects=True, vmem_limit_bytes=60 * 2**20
        ),
    )(tokens, weight_codes, weight_exp, grad_exp, recast_exp, out_grad)


def solution(mesh):
    placed = (
        P(("group", "inner"), None),
        P("inner", None),
        P(),
        P(),
        P(),
        P(("group", "inner"), None),
    )
    return jax.shard_map(
        body,
        mesh=mesh,
        in_specs=placed,
        out_specs=(P(("group", "inner"), None), P(("inner", "group"), None)),
        check_vma=False,
    )
```

```python
import jax
import jax.numpy as jnp
from jax import lax
from jax.experimental import pallas as pl
from jax.experimental.pallas import tpu as pltpu
from jax.sharding import PartitionSpec as P

code_limit = 448.0
MESH = pl.DeviceIdType.MESH
NX, NY, NZ, RUN = 4, 4, 32, 8
QB, TOK = 128, 192


def mod(a, n):
    return lax.rem(a + 2 * n, n)


def coords():
    g = lax.axis_index("group")
    i = lax.axis_index("inner")
    return i // 16, g // 4, (g % 4) * RUN + (i // 2) % RUN, i % 2


def dev(x, y, z, c):
    x, y, z = mod(x, NX), mod(y, NY), mod(z, NZ)
    return (y * (NZ // RUN) + z // RUN, (x * RUN + z % RUN) * 2 + c)


def pow2(e):
    return jnp.left_shift(jnp.int32(1), e + 15).astype(jnp.float32) * (2.0**-15)


def block(x, zl, c):
    return (x * RUN + zl) * 2 + c


def kernel(
    tok_hbm, codes_hbm, wexp_hbm, gexp_hbm, rexp_hbm, og_hbm,
    act_out, grad_out,
    tok, codes, og, wexp, gexp, rexp,
    wbuf, dt, cod, sibin, xout, xin, zout, zin, pout, pin,
    load_sem,
    gz_s, gz_r, gx_s, gx_r, gy_s, gy_r, gc_s, gc_r,
    sib_s, sib_r, rx_s, rx_r, rz_s, rz_r, p_s, p_r,
    know1, know2,
):
    x, y, z, c = coords()
    zl = z % RUN
    run0 = z - zl

    loads = [
        pltpu.make_async_copy(src, dst, load_sem.at[k])
        for k, (src, dst) in enumerate(
            ((codes_hbm, codes), (wexp_hbm, wexp), (gexp_hbm, gexp), (rexp_hbm, rexp), (og_hbm, og), (tok_hbm, tok))
        )
    ]
    for copy in loads:
        copy.start()

    barrier = pltpu.get_barrier_semaphore()
    near = [dev(x, y, z + d, c) for d in (2, -2)]
    near += [dev(x + 2, y, z, c)]
    near += [dev(x, y, z + d, c) for d in (1, -1)]
    near += [dev(x + d, y, z, c) for d in (1, 3)]
    near += [dev(x, y + d, z, c) for d in (1, 2, 3)]
    near += [dev(x, y, z, 1 - c)]
    for who in near:
        pl.semaphore_signal(barrier, inc=1, device_id=who, device_id_type=MESH)

    loads[0].wait()
    loads[1].wait()
    own = codes[...].astype(jnp.float32) * pow2(wexp[block(x, zl, c)])
    wbuf[zl, x, c] = own.astype(jnp.bfloat16)
    pl.semaphore_wait(barrier, len(near))

    odd = (zl + y) % 2

    def origin(k, odd):
        straight = jnp.where(k == 3, 4, jnp.where(k == 2, -2, 2 * k))
        crossed = (k // 2 * 2 + 1) * (1 - 2 * (k % 2))
        return mod(zl + jnp.where(odd == 1, crossed, straight), RUN)

    def gz(n, far, k, zs):
        slot = wbuf.at[zs, x, c]
        return pltpu.make_async_remote_copy(
            src_ref=slot, dst_ref=slot, send_sem=gz_s.at[n], recv_sem=gz_r.at[k],
            device_id=dev(x, y, z + far, c), device_id_type=MESH,
        )

    def gz_wait(k):
        slot = wbuf.at[origin(k, odd), x, c]
        pltpu.make_async_remote_copy(
            src_ref=slot, dst_ref=slot, send_sem=gz_s.at[k], recv_sem=gz_r.at[k],
            device_id=dev(x, y, z + 1, c), device_id_type=MESH,
        ).wait_recv()

    def gx(k, d, shift):
        slot = wbuf.at[origin(k, odd), mod(x + shift, NX), c]
        return pltpu.make_async_remote_copy(
            src_ref=slot, dst_ref=slot, send_sem=gx_s.at[k, d - 1], recv_sem=gx_r.at[k, d - 1],
            device_id=dev(x + d, y, z, c), device_id_type=MESH,
        )

    def gy(k, xs, odd):
        slot = wbuf.at[origin(k, odd), xs, c]
        return pltpu.make_async_remote_copy(
            src_ref=slot, dst_ref=slot, send_sem=gy_s.at[k, xs], recv_sem=gy_r.at[k, xs],
            device_id=dev(x, y + 1 - 2 * (xs % 2), z, c), device_id_type=MESH,
        )

    def gc(zs, xs, cs):
        slot = wbuf.at[zs, xs, cs]
        return pltpu.make_async_remote_copy(
            src_ref=slot, dst_ref=slot, send_sem=gc_s.at[zs, xs], recv_sem=gc_r.at[zs, xs],
            device_id=dev(x, y, z, 1 - c), device_id_type=MESH,
        )

    def each(n, f):
        lax.fori_loop(0, n, lambda k, _: (f(k), 0)[1], 0)

    forth = (x + c) % 2 == 0
    from_own = [gz(n, far, k, zl) for n, (far, k) in enumerate(((2, 2), (-2, 1), (1, 1), (-1, 0)))]
    above, below = mod(zl + 2, RUN), mod(zl - 2, RUN)
    passed = [gz(4, -1, 2, above), gz(5, 1, 3, below)]
    passed_far = gz(6, jnp.where(forth, 2, -2), 3, jnp.where(forth, below, above))

    @pl.when(odd == 0)
    def _():
        for copy in from_own:
            copy.start()

    @pl.when(odd == 1)
    def _():
        gc(zl, x, c).start()

    def arrived_z(k):
        @pl.when((odd == 1) | (k > 0))
        def _():
            gz_wait(k)

        @pl.when((odd == 0) & (k == 1))
        def _():
            passed[0].start()

            @pl.when(jnp.logical_not(forth))
            def _():
                passed_far.start()

        @pl.when((odd == 0) & (k == 2))
        def _():
            passed[1].start()

            @pl.when(forth)
            def _():
                passed_far.start()

        for d in (2, 1, 3):
            gx(k, d, 0).start()

        @pl.when((odd == 1) | (k > 0))
        def _():
            gy(k, x, odd).start()

        gc(origin(k, odd), x, c).start()

    def arrived_x(k):
        for d in (1, 3, 2):
            gx(k, d, -d).wait_recv()
            gy(k, mod(x - d, NX), odd).start()
            gc(origin(k, odd), mod(x - d, NX), c).start()

    def gather(k):
        @pl.when(k >= 3)
        def _():
            arrived_x(k - 3)

        @pl.when(k < 4)
        def _():
            arrived_z(k)

    each(7, gather)

    def arrived_y(k):
        for xs in range(NX):
            @pl.when((odd == 0) | (k > 0) | (xs != x))
            def _():
                gy(k, xs, 1 - odd).wait_recv()
                gc(origin(k, 1 - odd), xs, c).start()

    each(4, arrived_y)

    for copy in loads[2:]:
        copy.wait()

    for d in (4, -4):
        pl.semaphore_signal(know1, inc=1, device_id=dev(x, y, z + d, c), device_id_type=MESH)

    def product(k, acc):
        zs = origin(k % 4, lax.rem(odd + k // 4, 2))
        for xs in range(NX):
            gc(zs, xs, 1 - c).wait_recv()
        for xs in range(NX):
            cols = pl.ds(pl.multiple_of((xs * RUN + zs) * 256, 256), 256)
            w = wbuf[zs, xs].reshape(2 * QB, QB)
            acc += jnp.dot(tok[:, cols], w, preferred_element_type=jnp.float32)
        return acc

    pre = lax.fori_loop(0, RUN, product, jnp.zeros((TOK, QB), jnp.float32))
    sig = jax.nn.sigmoid(pre)
    act_out[...] = (pre * sig).astype(jnp.bfloat16)
    delta = og[...].astype(jnp.float32) * sig * (1.0 + pre * (1.0 - sig))
    dt[...] = delta.astype(jnp.bfloat16).T

    rest = RUN - 1
    up = zl * 2 < rest
    top = jnp.minimum(zl, rest - 1)
    short, long = jnp.where(up, top, rest - 1 - top), jnp.where(up, rest - 1 - top, top)

    def place(k):
        n = k - 1
        both = n - (long - short)
        far = jnp.where(both < 0, long - n, short - both // 2)
        ahead = up ^ ((both >= 0) & (both % 2 == 1))
        return jnp.where(n < 0, 7 - k, jnp.where(zl < rest, top + jnp.where(ahead, far, -far), n))

    early = zl >= rest
    mine_at = jnp.where(early, 7 - zl, 7)

    def sib(k, side):
        return pltpu.make_async_remote_copy(
            src_ref=cod.at[k, side], dst_ref=sibin.at[k], send_sem=sib_s.at[k], recv_sem=sib_r.at[k],
            device_id=dev(x, y, z, 1 - c), device_id_type=MESH,
        )

    def rx(k, d):
        return pltpu.make_async_remote_copy(
            src_ref=xout.at[k, mod(x + d, NX)], dst_ref=xin.at[k, d - 1], send_sem=rx_s.at[k, d - 1],
            recv_sem=rx_r.at[k, d - 1], device_id=dev(x + d, y, z, c), device_id_type=MESH,
        )

    def rz(k):
        return pltpu.make_async_remote_copy(
            src_ref=zout.at[k], dst_ref=zin.at[zl], send_sem=rz_s.at[k], recv_sem=rz_r.at[zl],
            device_id=dev(x, y, run0 + place(k), c), device_id_type=MESH,
        )

    def rz_wait(there):
        pltpu.make_async_remote_copy(
            src_ref=zout.at[0], dst_ref=zin.at[there], send_sem=rz_s.at[0], recv_sem=rz_r.at[there],
            device_id=dev(x, y, run0 + there, c), device_id_type=MESH,
        ).wait_recv()

    def coded(k):
        zs = 7 - place(k)
        for xs in range(NX):
            cols = pl.ds(pl.multiple_of((xs * RUN + zs) * 256, 256), 256)
            part = jnp.dot(dt[...], tok[:, cols], preferred_element_type=jnp.float32)
            for cs in range(2):
                scaled = part[:, cs * QB:(cs + 1) * QB] * pow2(-gexp[block(xs, zs, cs)])
                cod[k, cs, xs] = jnp.clip(scaled, -code_limit, code_limit).astype(jnp.bfloat16)
        sib(k, 1 - c).start()

    def over_cores(k):
        sib(k, 1 - c).wait_recv()
        for xs in range(NX):
            both = cod[k, c, xs].astype(jnp.float32) + sibin[k, xs].astype(jnp.float32)
            xout[k, xs] = both.astype(jnp.bfloat16)
        for d in (2, 1, 3):
            rx(k, d).start()

    def over_x(k):
        total = xout[k, x].astype(jnp.float32)
        for d in (1, 3, 2):
            rx(k, d).wait_recv()
            total += xin[k, d - 1].astype(jnp.float32)
        zout[k] = total.astype(jnp.bfloat16)

        @pl.when(place(k) != zl)
        def _():
            rz(k).start()

    def stage(k):
        @pl.when(k < 8)
        def _():
            coded(k)

        @pl.when((k >= 1) & (k < 9))
        def _():
            over_cores(k - 1)

        @pl.when(k == 2)
        def _():
            pl.semaphore_wait(know1, 2)
            for d in (8, -8):
                pl.semaphore_signal(know2, inc=1, device_id=dev(x, y, z + d, c), device_id_type=MESH)

        @pl.when(k >= 2)
        def _():
            over_x(k - 2)

    mirror = 7 - zl

    def piece(k):
        dy = jnp.where(k % 4 == 0, 2, jnp.where(k % 4 == 3, 0, 2 * (k % 4) - 1))
        side = jnp.where(zl < 4, 1, 3)
        dz = jnp.where(k // 4 == 0, 2, jnp.where(k // 4 == 1, side, jnp.where(k // 4 == 2, 0, 4 - side)))
        there = mod(y + dy, NY) * 4 + mod(z // RUN + dz, 4)
        return pltpu.make_async_remote_copy(
            src_ref=pout.at[there], dst_ref=pin.at[k], send_sem=p_s.at[k], recv_sem=p_r.at[k],
            device_id=(there, block(x, mirror, c)), device_id_type=MESH,
        )

    def over_run():
        def add_z(k, acc):
            there = lax.rem(zl + 1 + k, RUN)
            rz_wait(there)
            return acc + zin[there].astype(jnp.float32)

        first = lax.fori_loop(0, 7, add_z, zout[mine_at].astype(jnp.float32))
        recoded = jnp.clip(first * pow2(-rexp[block(x, mirror, c)]), -code_limit, code_limit)
        recoded = recoded.astype(jnp.bfloat16).astype(jnp.float32)
        pout[...] = recoded.T.reshape(16, 8, QB)
        pl.semaphore_wait(know2, 2)
        each(16, lambda k: piece(k).start())

    def step(k):
        stage(k)

        @pl.when(k == jnp.where(early, 8, 9))
        def _():
            over_run()

    each(10, step)

    def add_piece(k, acc):
        piece(k).wait_recv()
        return acc + pin[k]

    summed = lax.fori_loop(0, 16, add_piece, jnp.zeros((8, QB), jnp.float32))
    mine = block(x, zl, c)
    grad_out[...] = summed * pow2(gexp[mine] + rexp[mine])

    @pl.when(odd == 0)
    def _():
        for copy in from_own + passed + [passed_far]:
            copy.wait_send()

    def sent4(k):
        for d in (1, 2, 3):
            gx(k, d, 0).wait_send()
        for xs in range(NX):
            @pl.when((odd == 1) | (k > 0) | (xs != x))
            def _():
                gy(k, xs, odd).wait_send()

    each(4, sent4)
    each(32, lambda k: gc(k // NX, k % NX, c).wait_send())

    def sent8(k):
        for d in (1, 2, 3):
            rx(k, d).wait_send()
        sib(k, 1 - c).wait_send()

    each(8, sent8)

    def sent_z(k):
        @pl.when(place(k) != zl)
        def _():
            rz(k).wait_send()

    each(8, sent_z)
    each(16, lambda k: piece(k).wait_send())


def body(tokens, weight_codes, weight_exp, grad_exp, recast_exp, out_grad):
    bf, f32 = jnp.bfloat16, jnp.float32
    dma, vmem = pltpu.SemaphoreType.DMA, pltpu.VMEM
    return pl.pallas_call(
        kernel,
        name="mlp_block",
        out_shape=(vmem((TOK, QB), bf), vmem((8, QB), f32)),
        in_specs=[pl.BlockSpec(memory_space=pltpu.HBM)] * 6,
        out_specs=(pl.BlockSpec(memory_space=pltpu.VMEM), pl.BlockSpec(memory_space=pltpu.VMEM)),
        scratch_shapes=[
            vmem((TOK, 8192), bf), vmem((QB, QB), bf), vmem((TOK, QB), bf),
            pltpu.SMEM((64,), jnp.int32), pltpu.SMEM((64,), jnp.int32), pltpu.SMEM((64,), jnp.int32),
            vmem((RUN, NX, 2, QB, QB), bf), vmem((QB, TOK), bf),
            vmem((RUN, 2, NX, QB, QB), bf), vmem((RUN, NX, QB, QB), bf),
            vmem((RUN, NX, QB, QB), bf), vmem((RUN, 3, QB, QB), bf),
            vmem((RUN, QB, QB), bf), vmem((RUN, QB, QB), bf),
            vmem((16, 8, QB), f32), vmem((16, 8, QB), f32),
            dma((6,)),
            dma((7,)), dma((4,)), dma((4, 3)), dma((4, 3)), dma((4, 4)), dma((4, 4)), dma((8, 4)), dma((8, 4)),
            dma((8,)), dma((8,)), dma((8, 3)), dma((8, 3)), dma((8,)), dma((8,)), dma((16,)), dma((16,)),
            pltpu.SemaphoreType.REGULAR, pltpu.SemaphoreType.REGULAR,
        ],
        compiler_params=pltpu.CompilerParams(
            collective_id=0, has_side_effects=True, vmem_limit_bytes=60 * 2**20
        ),
    )(tokens, weight_codes, weight_exp, grad_exp, recast_exp, out_grad)


def solution(mesh):
    placed = (
        P(("group", "inner"), None),
        P("inner", None),
        P(),
        P(),
        P(),
        P(("group", "inner"), None),
    )
    return jax.shard_map(
        body,
        mesh=mesh,
        in_specs=placed,
        out_specs=(P(("group", "inner"), None), P(("inner", "group"), None)),
        check_vma=False,
    )
```

```python
import jax
import jax.numpy as jnp
from jax import lax
from jax.experimental import pallas as pl
from jax.experimental.pallas import tpu as pltpu
from jax.sharding import PartitionSpec as P

code_limit = 448.0
MESH = pl.DeviceIdType.MESH
NX, NY, NZ, RUN = 4, 4, 32, 8
QB, TOK = 128, 192


def mod(a, n):
    return lax.rem(a + 2 * n, n)


def coords():
    g = lax.axis_index("group")
    i = lax.axis_index("inner")
    return i // 16, g // 4, (g % 4) * RUN + (i // 2) % RUN, i % 2


def dev(x, y, z, c):
    x, y, z = mod(x, NX), mod(y, NY), mod(z, NZ)
    return (y * (NZ // RUN) + z // RUN, (x * RUN + z % RUN) * 2 + c)


def pow2(e):
    return jnp.left_shift(jnp.int32(1), e + 15).astype(jnp.float32) * (2.0**-15)


def block(x, zl, c):
    return (x * RUN + zl) * 2 + c


def kernel(
    tok_hbm, codes_hbm, wexp_hbm, gexp_hbm, rexp_hbm, og_hbm,
    act_out, grad_out,
    tok, codes, og, wexp, gexp, rexp,
    wbuf, dt, cod, sibin, xout, xin, zout, zin, pout, pin,
    load_sem,
    gz_s, gz_r, gx_s, gx_r, gy_s, gy_r, gc_s, gc_r,
    sib_s, sib_r, rx_s, rx_r, rz_s, rz_r, p_s, p_r,
    know0, know1, know2,
):
    x, y, z, c = coords()
    zl = z % RUN

    loads = [
        pltpu.make_async_copy(src, dst, load_sem.at[k])
        for k, (src, dst) in enumerate(
            ((codes_hbm, codes), (wexp_hbm, wexp), (gexp_hbm, gexp), (rexp_hbm, rexp), (og_hbm, og), (tok_hbm, tok))
        )
    ]
    for copy in loads:
        copy.start()

    barrier = pltpu.get_barrier_semaphore()
    near = [dev(x, y, z + d, c) for d in (2, -2)]
    near += [dev(x + 2, y, z, c)]
    near += [dev(x, y, z + d, c) for d in (1, -1)]
    near += [dev(x + d, y, z, c) for d in (1, 3)]
    near += [dev(x, y + d, z, c) for d in (1, 2, 3)]
    near += [dev(x, y, z, 1 - c)]
    for who in near:
        pl.semaphore_signal(barrier, inc=1, device_id=who, device_id_type=MESH)

    loads[0].wait()
    loads[1].wait()
    own = codes[...].astype(jnp.float32) * pow2(wexp[block(x, zl, c)])
    wbuf[zl, x, c] = own.astype(jnp.bfloat16)
    pl.semaphore_wait(barrier, len(near))

    group, inner = lax.axis_index("group"), lax.axis_index("inner")
    other = (group, inner + 1 - 2 * c)
    along_x = {d: dev(x + d, y, z, c) for d in (1, 2, 3)}
    up_y, down_y = dev(x, y + 1, z, c)[0], dev(x, y - 1, z, c)[0]

    odd = (zl + y) % 2

    def origin(k, odd):
        straight = jnp.where(k == 3, 4, jnp.where(k == 2, -2, 2 * k))
        crossed = (k // 2 * 2 + 1) * (1 - 2 * (k % 2))
        return mod(zl + jnp.where(odd == 1, crossed, straight), RUN)

    def gz(n, far, k, zs):
        slot = wbuf.at[zs, x, c]
        return pltpu.make_async_remote_copy(
            src_ref=slot, dst_ref=slot, send_sem=gz_s.at[n], recv_sem=gz_r.at[k],
            device_id=dev(x, y, z + far, c), device_id_type=MESH,
        )

    def gz_wait(k):
        slot = wbuf.at[origin(k, odd), x, c]
        pltpu.make_async_remote_copy(
            src_ref=slot, dst_ref=slot, send_sem=gz_s.at[k], recv_sem=gz_r.at[k],
            device_id=other, device_id_type=MESH,
        ).wait_recv()

    def gx(k, d, shift):
        slot = wbuf.at[origin(k, odd), mod(x + shift, NX), c]
        return pltpu.make_async_remote_copy(
            src_ref=slot, dst_ref=slot, send_sem=gx_s.at[k, d - 1], recv_sem=gx_r.at[k, d - 1],
            device_id=along_x[d], device_id_type=MESH,
        )

    def gy(k, xs, odd):
        slot = wbuf.at[origin(k, odd), xs, c]
        return pltpu.make_async_remote_copy(
            src_ref=slot, dst_ref=slot, send_sem=gy_s.at[k, xs], recv_sem=gy_r.at[k, xs],
            device_id=(jnp.where(xs % 2 == 0, up_y, down_y), inner), device_id_type=MESH,
        )

    def gc(zs, xs, cs):
        slot = wbuf.at[zs, xs, cs]
        return pltpu.make_async_remote_copy(
            src_ref=slot, dst_ref=slot, send_sem=gc_s.at[zs, xs], recv_sem=gc_r.at[zs, xs],
            device_id=other, device_id_type=MESH,
        )

    def each(n, f):
        lax.fori_loop(0, n, lambda k, _: (f(k), 0)[1], 0)

    forth = (x + c) % 2 == 0
    from_own = [gz(n, far, k, zl) for n, (far, k) in enumerate(((2, 2), (-2, 1), (1, 1), (-1, 0)))]
    above, below = mod(zl + 2, RUN), mod(zl - 2, RUN)
    passed = [gz(4, -1, 2, above), gz(5, 1, 3, below)]
    passed_far = gz(6, jnp.where(forth, 2, -2), 3, jnp.where(forth, below, above))

    @pl.when(odd == 0)
    def _():
        for copy in from_own:
            copy.start()

    @pl.when(odd == 1)
    def _():
        gc(zl, x, c).start()

    def arrived_z(k):
        @pl.when((odd == 1) | (k > 0))
        def _():
            gz_wait(k)

        @pl.when((odd == 0) & (k == 1))
        def _():
            passed[0].start()

            @pl.when(jnp.logical_not(forth))
            def _():
                passed_far.start()

        @pl.when((odd == 0) & (k == 2))
        def _():
            passed[1].start()

            @pl.when(forth)
            def _():
                passed_far.start()

        for d in (2, 1, 3):
            gx(k, d, 0).start()

        @pl.when((odd == 1) | (k > 0))
        def _():
            gy(k, x, odd).start()

        gc(origin(k, odd), x, c).start()

    def arrived_x(k):
        for d in (1, 3, 2):
            gx(k, d, -d).wait_recv()
            gy(k, mod(x - d, NX), odd).start()
            gc(origin(k, odd), mod(x - d, NX), c).start()

    def gather(k):
        @pl.when(k >= 3)
        def _():
            arrived_x(k - 3)

        @pl.when(k < 4)
        def _():
            arrived_z(k)

    each(7, gather)
    for d in (4, -4):
        pl.semaphore_signal(know0, inc=1, device_id=dev(x, y, z + d, c), device_id_type=MESH)

    def arrived_y(k):
        for xs in range(NX):
            @pl.when((odd == 0) | (k > 0) | (xs != x))
            def _():
                gy(k, xs, 1 - odd).wait_recv()
                gc(origin(k, 1 - odd), xs, c).start()

    each(4, arrived_y)

    for copy in loads[2:]:
        copy.wait()

    for d in (4, -4):
        pl.semaphore_signal(know1, inc=1, device_id=dev(x, y, z + d, c), device_id_type=MESH)

    def product(k, acc):
        zs = origin(k % 4, lax.rem(odd + k // 4, 2))
        for xs in range(NX):
            gc(zs, xs, 1 - c).wait_recv()
        for xs in range(NX):
            cols = pl.ds(pl.multiple_of((xs * RUN + zs) * 256, 256), 256)
            w = wbuf[zs, xs].reshape(2 * QB, QB)
            acc += jnp.dot(tok[:, cols], w, preferred_element_type=jnp.float32)
        return acc

    pre = lax.fori_loop(0, RUN, product, jnp.zeros((TOK, QB), jnp.float32))
    sig = jax.nn.sigmoid(pre)
    act_out[...] = (pre * sig).astype(jnp.bfloat16)
    delta = og[...].astype(jnp.float32) * sig * (1.0 + pre * (1.0 - sig))
    dt[...] = delta.astype(jnp.bfloat16).T

    rest = RUN - 1
    up = zl * 2 < rest
    top = jnp.minimum(zl, rest - 1)
    short, long = jnp.where(up, top, rest - 1 - top), jnp.where(up, rest - 1 - top, top)

    def place(k):
        n = k - 1
        both = n - (long - short)
        far = jnp.where(both < 0, long - n, short - both // 2)
        ahead = up ^ ((both >= 0) & (both % 2 == 1))
        return jnp.where(n < 0, 7 - k, jnp.where(zl < rest, top + jnp.where(ahead, far, -far), n))

    early = zl >= rest
    mine_at = jnp.where(early, 7 - zl, 7)

    def sib(k, side):
        return pltpu.make_async_remote_copy(
            src_ref=cod.at[k, side], dst_ref=sibin.at[k], send_sem=sib_s.at[k], recv_sem=sib_r.at[k],
            device_id=other, device_id_type=MESH,
        )

    def rx(k, d):
        return pltpu.make_async_remote_copy(
            src_ref=xout.at[k, mod(x + d, NX)], dst_ref=xin.at[k, d - 1], send_sem=rx_s.at[k, d - 1],
            recv_sem=rx_r.at[k, d - 1], device_id=along_x[d], device_id_type=MESH,
        )

    def rz(k):
        return pltpu.make_async_remote_copy(
            src_ref=zout.at[k], dst_ref=zin.at[zl], send_sem=rz_s.at[k], recv_sem=rz_r.at[zl],
            device_id=(group, block(x, place(k), c)), device_id_type=MESH,
        )

    def rz_wait(there):
        pltpu.make_async_remote_copy(
            src_ref=zout.at[0], dst_ref=zin.at[there], send_sem=rz_s.at[0], recv_sem=rz_r.at[there],
            device_id=other, device_id_type=MESH,
        ).wait_recv()

    def coded(k):
        zs = 7 - place(k)
        for xs in range(NX):
            cols = pl.ds(pl.multiple_of((xs * RUN + zs) * 256, 256), 256)
            part = jnp.dot(dt[...], tok[:, cols], preferred_element_type=jnp.float32)
            for cs in range(2):
                scaled = part[:, cs * QB:(cs + 1) * QB] * pow2(-gexp[block(xs, zs, cs)])
                cod[k, cs, xs] = jnp.clip(scaled, -code_limit, code_limit).astype(jnp.bfloat16)
        sib(k, 1 - c).start()

    def over_cores(k):
        sib(k, 1 - c).wait_recv()
        for xs in range(NX):
            both = cod[k, c, xs].astype(jnp.float32) + sibin[k, xs].astype(jnp.float32)
            xout[k, xs] = both.astype(jnp.bfloat16)
        for d in (2, 1, 3):
            rx(k, d).start()

    def over_x(k):
        total = xout[k, x].astype(jnp.float32)
        for d in (1, 3, 2):
            rx(k, d).wait_recv()
            total += xin[k, d - 1].astype(jnp.float32)
        zout[k] = total.astype(jnp.bfloat16)

        @pl.when(place(k) != zl)
        def _():
            rz(k).start()

    def front(k):
        @pl.when(k < 8)
        def _():
            coded(k)

        @pl.when(k >= 4)
        def _():
            over_cores(k - 4)

    each(12, front)

    mirror = 7 - zl

    def piece(k):
        dy = jnp.where(k % 4 == 0, 2, jnp.where(k % 4 == 3, 0, 2 * (k % 4) - 1))
        side = jnp.where(zl < 4, 1, 3)
        dz = jnp.where(k // 4 == 0, 2, jnp.where(k // 4 == 1, side, jnp.where(k // 4 == 2, 0, 4 - side)))
        there = mod(y + dy, NY) * 4 + mod(z // RUN + dz, 4)
        return pltpu.make_async_remote_copy(
            src_ref=pout.at[there], dst_ref=pin.at[k], send_sem=p_s.at[k], recv_sem=p_r.at[k],
            device_id=(there, block(x, mirror, c)), device_id_type=MESH,
        )

    def over_run():
        def add_z(k, acc):
            there = lax.rem(zl + 1 + k, RUN)
            rz_wait(there)
            return acc + zin[there].astype(jnp.float32)

        first = lax.fori_loop(0, 7, add_z, zout[mine_at].astype(jnp.float32))
        recoded = jnp.clip(first * pow2(-rexp[block(x, mirror, c)]), -code_limit, code_limit)
        recoded = recoded.astype(jnp.bfloat16).astype(jnp.float32)
        pout[...] = recoded.T.reshape(16, 8, QB)
        pl.semaphore_wait(know2, 2)
        each(16, lambda k: piece(k).start())

    def back(k):
        @pl.when(k == 0)
        def _():
            pl.semaphore_wait(know0, 2)

        @pl.when(k == 2)
        def _():
            pl.semaphore_wait(know1, 2)
            for d in (8, -8):
                pl.semaphore_signal(know2, inc=1, device_id=dev(x, y, z + d, c), device_id_type=MESH)

        over_x(k)

        @pl.when(k == jnp.where(early, 7, 7))
        def _():
            over_run()

    each(8, back)

    @pl.when(odd == 0)
    def _():
        for copy in from_own + passed + [passed_far]:
            copy.wait_send()

    def sent4(k):
        for d in (1, 2, 3):
            gx(k, d, 0).wait_send()
        for xs in range(NX):
            @pl.when((odd == 1) | (k > 0) | (xs != x))
            def _():
                gy(k, xs, odd).wait_send()

    each(4, sent4)
    each(32, lambda k: gc(k // NX, k % NX, c).wait_send())

    def sent8(k):
        for d in (1, 2, 3):
            rx(k, d).wait_send()
        sib(k, 1 - c).wait_send()

    each(8, sent8)

    def sent_z(k):
        @pl.when(place(k) != zl)
        def _():
            rz(k).wait_send()

    each(8, sent_z)
    each(16, lambda k: piece(k).wait_send())

    def add_piece(k, acc):
        piece(k).wait_recv()
        return acc + pin[k]

    summed = lax.fori_loop(0, 16, add_piece, jnp.zeros((8, QB), jnp.float32))
    mine = block(x, zl, c)
    grad_out[...] = summed * pow2(gexp[mine] + rexp[mine])


def body(tokens, weight_codes, weight_exp, grad_exp, recast_exp, out_grad):
    bf, f32 = jnp.bfloat16, jnp.float32
    dma, vmem = pltpu.SemaphoreType.DMA, pltpu.VMEM
    return pl.pallas_call(
        kernel,
        name="mlp_block",
        out_shape=(vmem((TOK, QB), bf), vmem((8, QB), f32)),
        in_specs=[pl.BlockSpec(memory_space=pltpu.HBM)] * 6,
        out_specs=(pl.BlockSpec(memory_space=pltpu.VMEM), pl.BlockSpec(memory_space=pltpu.VMEM)),
        scratch_shapes=[
            vmem((TOK, 8192), bf), vmem((QB, QB), bf), vmem((TOK, QB), bf),
            pltpu.SMEM((64,), jnp.int32), pltpu.SMEM((64,), jnp.int32), pltpu.SMEM((64,), jnp.int32),
            vmem((RUN, NX, 2, QB, QB), bf), vmem((QB, TOK), bf),
            vmem((RUN, 2, NX, QB, QB), bf), vmem((RUN, NX, QB, QB), bf),
            vmem((RUN, NX, QB, QB), bf), vmem((RUN, 3, QB, QB), bf),
            vmem((RUN, QB, QB), bf), vmem((RUN, QB, QB), bf),
            vmem((16, 8, QB), f32), vmem((16, 8, QB), f32),
            dma((6,)),
            dma((7,)), dma((4,)), dma((4, 3)), dma((4, 3)), dma((4, 4)), dma((4, 4)), dma((8, 4)), dma((8, 4)),
            dma((8,)), dma((8,)), dma((8, 3)), dma((8, 3)), dma((8,)), dma((8,)), dma((16,)), dma((16,)),
            pltpu.SemaphoreType.REGULAR, pltpu.SemaphoreType.REGULAR, pltpu.SemaphoreType.REGULAR,
        ],
        compiler_params=pltpu.CompilerParams(
            collective_id=0, has_side_effects=True, vmem_limit_bytes=60 * 2**20
        ),
    )(tokens, weight_codes, weight_exp, grad_exp, recast_exp, out_grad)


def solution(mesh):
    placed = (
        P(("group", "inner"), None),
        P("inner", None),
        P(),
        P(),
        P(),
        P(("group", "inner"), None),
    )
    return jax.shard_map(
        body,
        mesh=mesh,
        in_specs=placed,
        out_specs=(P(("group", "inner"), None), P(("inner", "group"), None)),
        check_vma=False,
    )
```

```python
import jax
import jax.numpy as jnp
from jax import lax
from jax.experimental import pallas as pl
from jax.experimental.pallas import tpu as pltpu
from jax.sharding import PartitionSpec as P

code_limit = 448.0
MESH = pl.DeviceIdType.MESH
NX, NY, NZ, RUN = 4, 4, 32, 8
QB, TOK = 128, 192


def mod(a, n):
    return lax.rem(a + 2 * n, n)


def coords():
    g = lax.axis_index("group")
    i = lax.axis_index("inner")
    return i // 16, g // 4, (g % 4) * RUN + (i // 2) % RUN, i % 2


def dev(x, y, z, c):
    x, y, z = mod(x, NX), mod(y, NY), mod(z, NZ)
    return (y * (NZ // RUN) + z // RUN, (x * RUN + z % RUN) * 2 + c)


def pow2(e):
    return jnp.left_shift(jnp.int32(1), e + 15).astype(jnp.float32) * (2.0**-15)


def block(x, zl, c):
    return (x * RUN + zl) * 2 + c


def kernel(
    tok_hbm, codes_hbm, wexp_hbm, gexp_hbm, rexp_hbm, og_hbm,
    act_out, grad_out,
    tok, codes, og, wexp, gexp, rexp,
    wbuf, dt, cod, sibin, xout, xin, zout, zin, zpair, pout, pin,
    load_sem,
    gz_s, gz_r, gx_s, gx_r, gy_s, gy_r, gc_s, gc_r,
    sib_s, sib_r, rx_s, rx_r, rz_s, rz_r, pair_r, p_s, p_r,
    know0, know1, know2,
):
    x, y, z, c = coords()
    zl = z % RUN

    loads = [
        pltpu.make_async_copy(src, dst, load_sem.at[k])
        for k, (src, dst) in enumerate(
            ((codes_hbm, codes), (wexp_hbm, wexp), (gexp_hbm, gexp), (rexp_hbm, rexp), (og_hbm, og), (tok_hbm, tok))
        )
    ]
    for copy in loads:
        copy.start()

    barrier = pltpu.get_barrier_semaphore()
    near = [dev(x, y, z + d, c) for d in (2, -2)]
    near += [dev(x + 2, y, z, c)]
    near += [dev(x, y, z + d, c) for d in (1, -1)]
    near += [dev(x + d, y, z, c) for d in (1, 3)]
    near += [dev(x, y + d, z, c) for d in (1, 2, 3)]
    near += [dev(x, y, z, 1 - c)]
    for who in near:
        pl.semaphore_signal(barrier, inc=1, device_id=who, device_id_type=MESH)

    loads[0].wait()
    loads[1].wait()
    own = codes[...].astype(jnp.float32) * pow2(wexp[block(x, zl, c)])
    wbuf[zl, x, c] = own.astype(jnp.bfloat16)
    pl.semaphore_wait(barrier, len(near))

    group, inner = lax.axis_index("group"), lax.axis_index("inner")
    other = (group, inner + 1 - 2 * c)
    along_x = {d: dev(x + d, y, z, c) for d in (1, 2, 3)}
    up_y, down_y = dev(x, y + 1, z, c)[0], dev(x, y - 1, z, c)[0]

    odd = (zl + y) % 2

    def origin(k, odd):
        straight = jnp.where(k == 3, 4, jnp.where(k == 2, -2, 2 * k))
        crossed = (k // 2 * 2 + 1) * (1 - 2 * (k % 2))
        return mod(zl + jnp.where(odd == 1, crossed, straight), RUN)

    def gz(n, far, k, zs):
        slot = wbuf.at[zs, x, c]
        return pltpu.make_async_remote_copy(
            src_ref=slot, dst_ref=slot, send_sem=gz_s.at[n], recv_sem=gz_r.at[k],
            device_id=dev(x, y, z + far, c), device_id_type=MESH,
        )

    def gz_wait(k):
        slot = wbuf.at[origin(k, odd), x, c]
        pltpu.make_async_remote_copy(
            src_ref=slot, dst_ref=slot, send_sem=gz_s.at[k], recv_sem=gz_r.at[k],
            device_id=other, device_id_type=MESH,
        ).wait_recv()

    def gx(k, d, shift):
        slot = wbuf.at[origin(k, odd), mod(x + shift, NX), c]
        return pltpu.make_async_remote_copy(
            src_ref=slot, dst_ref=slot, send_sem=gx_s.at[k, d - 1], recv_sem=gx_r.at[k, d - 1],
            device_id=along_x[d], device_id_type=MESH,
        )

    def gy(k, xs, odd):
        slot = wbuf.at[origin(k, odd), xs, c]
        return pltpu.make_async_remote_copy(
            src_ref=slot, dst_ref=slot, send_sem=gy_s.at[k, xs], recv_sem=gy_r.at[k, xs],
            device_id=(jnp.where(xs % 2 == 0, up_y, down_y), inner), device_id_type=MESH,
        )

    def gc(zs, xs, cs):
        slot = wbuf.at[zs, xs, cs]
        return pltpu.make_async_remote_copy(
            src_ref=slot, dst_ref=slot, send_sem=gc_s.at[zs, xs], recv_sem=gc_r.at[zs, xs],
            device_id=other, device_id_type=MESH,
        )

    def each(n, f):
        lax.fori_loop(0, n, lambda k, _: (f(k), 0)[1], 0)

    forth = (x + c) % 2 == 0
    from_own = [gz(n, far, k, zl) for n, (far, k) in enumerate(((2, 2), (-2, 1), (1, 1), (-1, 0)))]
    above, below = mod(zl + 2, RUN), mod(zl - 2, RUN)
    passed = [gz(4, -1, 2, above), gz(5, 1, 3, below)]
    passed_far = gz(6, jnp.where(forth, 2, -2), 3, jnp.where(forth, below, above))

    @pl.when(odd == 0)
    def _():
        for copy in from_own:
            copy.start()

    @pl.when(odd == 1)
    def _():
        gc(zl, x, c).start()

    def arrived_z(k):
        @pl.when((odd == 1) | (k > 0))
        def _():
            gz_wait(k)

        @pl.when((odd == 0) & (k == 1))
        def _():
            passed[0].start()

            @pl.when(jnp.logical_not(forth))
            def _():
                passed_far.start()

        @pl.when((odd == 0) & (k == 2))
        def _():
            passed[1].start()

            @pl.when(forth)
            def _():
                passed_far.start()

        for d in (2, 1, 3):
            gx(k, d, 0).start()

        @pl.when((odd == 1) | (k > 0))
        def _():
            gy(k, x, odd).start()

        gc(origin(k, odd), x, c).start()

    def arrived_x(k):
        for d in (1, 3, 2):
            gx(k, d, -d).wait_recv()
            gy(k, mod(x - d, NX), odd).start()
            gc(origin(k, odd), mod(x - d, NX), c).start()

    each(4, arrived_z)
    each(4, arrived_x)
    for d in (4, -4):
        pl.semaphore_signal(know0, inc=1, device_id=dev(x, y, z + d, c), device_id_type=MESH)

    def arrived_y(k):
        for xs in range(NX):
            @pl.when((odd == 0) | (k > 0) | (xs != x))
            def _():
                gy(k, xs, 1 - odd).wait_recv()
                gc(origin(k, 1 - odd), xs, c).start()

    each(4, arrived_y)

    for copy in loads[2:]:
        copy.wait()

    for d in (4, -4):
        pl.semaphore_signal(know1, inc=1, device_id=dev(x, y, z + d, c), device_id_type=MESH)

    def product(k, acc):
        zs = origin(k % 4, lax.rem(odd + k // 4, 2))
        for xs in range(NX):
            gc(zs, xs, 1 - c).wait_recv()
        for xs in range(NX):
            cols = pl.ds(pl.multiple_of((xs * RUN + zs) * 256, 256), 256)
            w = wbuf[zs, xs].reshape(2 * QB, QB)
            acc += jnp.dot(tok[:, cols], w, preferred_element_type=jnp.float32)
        return acc

    pre = lax.fori_loop(0, RUN, product, jnp.zeros((TOK, QB), jnp.float32))
    sig = jax.nn.sigmoid(pre)
    act_out[...] = (pre * sig).astype(jnp.bfloat16)
    delta = og[...].astype(jnp.float32) * sig * (1.0 + pre * (1.0 - sig))
    dt[...] = delta.astype(jnp.bfloat16).T

    spot, half = zl % 4, zl // 4
    there_half = 4 - 4 * half

    def across(n, parity):
        return there_half + 2 * jnp.where(half == 0, 1 - n, n) + parity

    def beside(n):
        last = jnp.where(spot < 2, 1 - spot, 5 - spot)
        return zl - spot + jnp.where(n == 2, last, jnp.where(spot < 2, 3 - n, n))

    def place(k):
        far = across(k % 2, jnp.where(k < 2, 1 - zl % 2, zl % 2))
        return jnp.where(k < 4, far, jnp.where(k < 7, beside(k - 4), zl))

    def sib(k, side):
        return pltpu.make_async_remote_copy(
            src_ref=cod.at[k, side], dst_ref=sibin.at[k], send_sem=sib_s.at[k], recv_sem=sib_r.at[k],
            device_id=other, device_id_type=MESH,
        )

    def rx(k, d):
        return pltpu.make_async_remote_copy(
            src_ref=xout.at[k, mod(x + d, NX)], dst_ref=xin.at[k, d - 1], send_sem=rx_s.at[k, d - 1],
            recv_sem=rx_r.at[k, d - 1], device_id=along_x[d], device_id_type=MESH,
        )

    def rz(k):
        return pltpu.make_async_remote_copy(
            src_ref=zout.at[k], dst_ref=zin.at[zl], send_sem=rz_s.at[k], recv_sem=rz_r.at[zl],
            device_id=(group, block(x, place(k), c)), device_id_type=MESH,
        )

    def pair(k):
        return pltpu.make_async_remote_copy(
            src_ref=zout.at[k], dst_ref=zpair.at[k], send_sem=rz_s.at[k], recv_sem=pair_r.at[k],
            device_id=(group, block(x, zl + 1 - 2 * (zl % 2), c)), device_id_type=MESH,
        )

    def rz_wait(there):
        pltpu.make_async_remote_copy(
            src_ref=zout.at[0], dst_ref=zin.at[there], send_sem=rz_s.at[0], recv_sem=rz_r.at[there],
            device_id=other, device_id_type=MESH,
        ).wait_recv()

    def coded(k):
        zs = 7 - place(k)
        for xs in range(NX):
            cols = pl.ds(pl.multiple_of((xs * RUN + zs) * 256, 256), 256)
            part = jnp.dot(dt[...], tok[:, cols], preferred_element_type=jnp.float32)
            for cs in range(2):
                scaled = part[:, cs * QB:(cs + 1) * QB] * pow2(-gexp[block(xs, zs, cs)])
                cod[k, cs, xs] = jnp.clip(scaled, -code_limit, code_limit).astype(jnp.bfloat16)
        sib(k, 1 - c).start()

    def over_cores(k):
        sib(k, 1 - c).wait_recv()
        for xs in range(NX):
            both = cod[k, c, xs].astype(jnp.float32) + sibin[k, xs].astype(jnp.float32)
            xout[k, xs] = both.astype(jnp.bfloat16)
        for d in (2, 1, 3):
            rx(k, d).start()

    def over_x(k):
        total = xout[k, x].astype(jnp.float32)
        for d in (1, 3, 2):
            rx(k, d).wait_recv()
            total += xin[k, d - 1].astype(jnp.float32)

        @pl.when((k == 2) | (k == 3))
        def _():
            pair(k - 2).wait_recv()
            zout[k] = (total + zpair[k - 2].astype(jnp.float32)).astype(jnp.bfloat16)

        @pl.when((k < 2) | (k > 3))
        def _():
            zout[k] = total.astype(jnp.bfloat16)

        @pl.when(k < 2)
        def _():
            pair(k).start()

        @pl.when((k > 1) & (k < 7))
        def _():
            rz(k).start()

    def front(k):
        @pl.when(k < 8)
        def _():
            coded(k)

        @pl.when(k >= 4)
        def _():
            over_cores(k - 4)

    each(12, front)

    mirror = 7 - zl

    def piece(k):
        dy = jnp.where(k % 4 == 0, 2, jnp.where(k % 4 == 3, 0, 2 * (k % 4) - 1))
        side = jnp.where(zl < 4, 1, 3)
        dz = jnp.where(k // 4 == 0, 2, jnp.where(k // 4 == 1, side, jnp.where(k // 4 == 2, 0, 4 - side)))
        there = mod(y + dy, NY) * 4 + mod(z // RUN + dz, 4)
        return pltpu.make_async_remote_copy(
            src_ref=pout.at[there], dst_ref=pin.at[k], send_sem=p_s.at[k], recv_sem=p_r.at[k],
            device_id=(there, block(x, mirror, c)), device_id_type=MESH,
        )

    def over_run():
        def add_z(k, acc):
            there = jnp.where(k < 2, across(k, zl % 2), beside(k - 2))
            rz_wait(there)
            return acc + zin[there].astype(jnp.float32)

        first = lax.fori_loop(0, 5, add_z, zout[7].astype(jnp.float32))
        recoded = jnp.clip(first * pow2(-rexp[block(x, mirror, c)]), -code_limit, code_limit)
        recoded = recoded.astype(jnp.bfloat16).astype(jnp.float32)
        pout[...] = recoded.T.reshape(16, 8, QB)
        pl.semaphore_wait(know2, 2)
        each(16, lambda k: piece(k).start())

    def back(k):
        @pl.when(k == 0)
        def _():
            pl.semaphore_wait(know0, 2)

        @pl.when(k == 2)
        def _():
            pl.semaphore_wait(know1, 2)
            for d in (8, -8):
                pl.semaphore_signal(know2, inc=1, device_id=dev(x, y, z + d, c), device_id_type=MESH)

        over_x(k)

    each(8, back)
    over_run()

    @pl.when(odd == 0)
    def _():
        for copy in from_own + passed + [passed_far]:
            copy.wait_send()

    def sent4(k):
        for d in (1, 2, 3):
            gx(k, d, 0).wait_send()
        for xs in range(NX):
            @pl.when((odd == 1) | (k > 0) | (xs != x))
            def _():
                gy(k, xs, odd).wait_send()

    each(4, sent4)
    each(32, lambda k: gc(k // NX, k % NX, c).wait_send())

    def sent8(k):
        for d in (1, 2, 3):
            rx(k, d).wait_send()
        sib(k, 1 - c).wait_send()

    each(8, sent8)

    def sent_z(k):
        @pl.when(k < 2)
        def _():
            pair(k).wait_send()

        @pl.when(k > 1)
        def _():
            rz(k).wait_send()

    each(7, sent_z)
    each(16, lambda k: piece(k).wait_send())

    def add_piece(k, acc):
        piece(k).wait_recv()
        return acc + pin[k]

    summed = lax.fori_loop(0, 16, add_piece, jnp.zeros((8, QB), jnp.float32))
    mine = block(x, zl, c)
    grad_out[...] = summed * pow2(gexp[mine] + rexp[mine])


def body(tokens, weight_codes, weight_exp, grad_exp, recast_exp, out_grad):
    bf, f32 = jnp.bfloat16, jnp.float32
    dma, vmem = pltpu.SemaphoreType.DMA, pltpu.VMEM
    return pl.pallas_call(
        kernel,
        name="mlp_block",
        out_shape=(vmem((TOK, QB), bf), vmem((8, QB), f32)),
        in_specs=[pl.BlockSpec(memory_space=pltpu.HBM)] * 6,
        out_specs=(pl.BlockSpec(memory_space=pltpu.VMEM), pl.BlockSpec(memory_space=pltpu.VMEM)),
        scratch_shapes=[
            vmem((TOK, 8192), bf), vmem((QB, QB), bf), vmem((TOK, QB), bf),
            pltpu.SMEM((64,), jnp.int32), pltpu.SMEM((64,), jnp.int32), pltpu.SMEM((64,), jnp.int32),
            vmem((RUN, NX, 2, QB, QB), bf), vmem((QB, TOK), bf),
            vmem((RUN, 2, NX, QB, QB), bf), vmem((RUN, NX, QB, QB), bf),
            vmem((RUN, NX, QB, QB), bf), vmem((RUN, 3, QB, QB), bf),
            vmem((RUN, QB, QB), bf), vmem((RUN, QB, QB), bf), vmem((2, QB, QB), bf),
            vmem((16, 8, QB), f32), vmem((16, 8, QB), f32),
            dma((6,)),
            dma((7,)), dma((4,)), dma((4, 3)), dma((4, 3)), dma((4, 4)), dma((4, 4)), dma((8, 4)), dma((8, 4)),
            dma((8,)), dma((8,)), dma((8, 3)), dma((8, 3)), dma((8,)), dma((8,)), dma((2,)), dma((16,)), dma((16,)),
            pltpu.SemaphoreType.REGULAR, pltpu.SemaphoreType.REGULAR, pltpu.SemaphoreType.REGULAR,
        ],
        compiler_params=pltpu.CompilerParams(
            collective_id=0, has_side_effects=True, vmem_limit_bytes=60 * 2**20
        ),
    )(tokens, weight_codes, weight_exp, grad_exp, recast_exp, out_grad)


def solution(mesh):
    placed = (
        P(("group", "inner"), None),
        P("inner", None),
        P(),
        P(),
        P(),
        P(("group", "inner"), None),
    )
    return jax.shard_map(
        body,
        mesh=mesh,
        in_specs=placed,
        out_specs=(P(("group", "inner"), None), P(("inner", "group"), None)),
        check_vma=False,
    )
```

```python
import jax
import jax.numpy as jnp
from jax import lax
from jax.experimental import pallas as pl
from jax.experimental.pallas import tpu as pltpu
from jax.sharding import PartitionSpec as P

code_limit = 448.0
MESH = pl.DeviceIdType.MESH
NX, NY, NZ, RUN = 4, 4, 32, 8
QB, TOK = 128, 192


def mod(a, n):
    return lax.rem(a + 2 * n, n)


def coords():
    g = lax.axis_index("group")
    i = lax.axis_index("inner")
    return i // 16, g // 4, (g % 4) * RUN + (i // 2) % RUN, i % 2


def dev(x, y, z, c):
    x, y, z = mod(x, NX), mod(y, NY), mod(z, NZ)
    return (y * (NZ // RUN) + z // RUN, (x * RUN + z % RUN) * 2 + c)


def pow2(e):
    return jnp.left_shift(jnp.int32(1), e + 15).astype(jnp.float32) * (2.0**-15)


def block(x, zl, c):
    return (x * RUN + zl) * 2 + c


def kernel(
    tok_hbm, codes_hbm, wexp_hbm, gexp_hbm, rexp_hbm, og_hbm,
    act_out, grad_out,
    tok, codes, og, wexp, gexp, rexp,
    wbuf, dt, cod, sibin, xout, xin, zout, zin, zpair, pout, pin,
    load_sem,
    gz_s, gz_r, gx_s, gx_r, gy_s, gy_r, gc_s, gc_r,
    sib_s, sib_r, rx_s, rx_r, rz_s, rz_r, pair_r, p_s, p_r,
    know0, know1, know2,
):
    x, y, z, c = coords()
    zl = z % RUN

    loads = [
        pltpu.make_async_copy(src, dst, load_sem.at[k])
        for k, (src, dst) in enumerate(
            ((codes_hbm, codes), (wexp_hbm, wexp), (gexp_hbm, gexp), (rexp_hbm, rexp), (og_hbm, og), (tok_hbm, tok))
        )
    ]
    for copy in loads:
        copy.start()

    barrier = pltpu.get_barrier_semaphore()
    near = [dev(x, y, z + d, c) for d in (2, -2)]
    near += [dev(x + 2, y, z, c)]
    near += [dev(x, y, z + d, c) for d in (1, -1)]
    near += [dev(x + d, y, z, c) for d in (1, 3)]
    near += [dev(x, y + d, z, c) for d in (1, 2, 3)]
    near += [dev(x, y, z, 1 - c)]
    for who in near:
        pl.semaphore_signal(barrier, inc=1, device_id=who, device_id_type=MESH)

    loads[0].wait()
    loads[1].wait()
    own = codes[...].astype(jnp.float32) * pow2(wexp[block(x, zl, c)])
    wbuf[zl, x, c] = own.astype(jnp.bfloat16)
    pl.semaphore_wait(barrier, len(near))

    group, inner = lax.axis_index("group"), lax.axis_index("inner")
    other = (group, inner + 1 - 2 * c)
    along_x = {d: dev(x + d, y, z, c) for d in (1, 2, 3)}
    up_y, down_y = dev(x, y + 1, z, c)[0], dev(x, y - 1, z, c)[0]

    odd = (zl + y) % 2

    def origin(k, odd):
        straight = jnp.where(k == 3, 4, jnp.where(k == 2, -2, 2 * k))
        crossed = (k // 2 * 2 + 1) * (1 - 2 * (k % 2))
        return mod(zl + jnp.where(odd == 1, crossed, straight), RUN)

    def gz(n, far, k, zs):
        slot = wbuf.at[zs, x, c]
        return pltpu.make_async_remote_copy(
            src_ref=slot, dst_ref=slot, send_sem=gz_s.at[n], recv_sem=gz_r.at[k],
            device_id=dev(x, y, z + far, c), device_id_type=MESH,
        )

    def gz_wait(k):
        slot = wbuf.at[origin(k, odd), x, c]
        pltpu.make_async_remote_copy(
            src_ref=slot, dst_ref=slot, send_sem=gz_s.at[k], recv_sem=gz_r.at[k],
            device_id=other, device_id_type=MESH,
        ).wait_recv()

    def gx(k, d, shift):
        slot = wbuf.at[origin(k, odd), mod(x + shift, NX), c]
        return pltpu.make_async_remote_copy(
            src_ref=slot, dst_ref=slot, send_sem=gx_s.at[k, d - 1], recv_sem=gx_r.at[k, d - 1],
            device_id=along_x[d], device_id_type=MESH,
        )

    def gy(k, xs, odd):
        slot = wbuf.at[origin(k, odd), xs, c]
        return pltpu.make_async_remote_copy(
            src_ref=slot, dst_ref=slot, send_sem=gy_s.at[k, xs], recv_sem=gy_r.at[k, xs],
            device_id=(jnp.where(xs % 2 == 0, up_y, down_y), inner), device_id_type=MESH,
        )

    def gc(zs, xs, cs):
        slot = wbuf.at[zs, xs, cs]
        return pltpu.make_async_remote_copy(
            src_ref=slot, dst_ref=slot, send_sem=gc_s.at[zs, xs], recv_sem=gc_r.at[zs, xs],
            device_id=other, device_id_type=MESH,
        )

    def each(n, f):
        lax.fori_loop(0, n, lambda k, _: (f(k), 0)[1], 0)

    forth = (x + c) % 2 == 0
    from_own = [gz(n, far, k, zl) for n, (far, k) in enumerate(((2, 2), (-2, 1), (1, 1), (-1, 0)))]
    above, below = mod(zl + 2, RUN), mod(zl - 2, RUN)
    passed = [gz(4, -1, 2, above), gz(5, 1, 3, below)]
    passed_far = gz(6, jnp.where(forth, 2, -2), 3, jnp.where(forth, below, above))

    @pl.when(odd == 0)
    def _():
        for copy in from_own:
            copy.start()

    @pl.when(odd == 1)
    def _():
        gc(zl, x, c).start()

    def arrived_z(k):
        @pl.when((odd == 1) | (k > 0))
        def _():
            gz_wait(k)

        @pl.when((odd == 0) & (k == 1))
        def _():
            passed[0].start()

            @pl.when(jnp.logical_not(forth))
            def _():
                passed_far.start()

        @pl.when((odd == 0) & (k == 2))
        def _():
            passed[1].start()

            @pl.when(forth)
            def _():
                passed_far.start()

        for d in (2, 1, 3):
            gx(k, d, 0).start()

        @pl.when((odd == 1) | (k > 0))
        def _():
            gy(k, x, odd).start()

        gc(origin(k, odd), x, c).start()

    def arrived_x(k):
        for d in (1, 3, 2):
            gx(k, d, -d).wait_recv()
            gy(k, mod(x - d, NX), odd).start()
            gc(origin(k, odd), mod(x - d, NX), c).start()

    for k in range(4):
        arrived_z(jnp.int32(k))
    for k in range(4):
        arrived_x(jnp.int32(k))
    for d in (4, -4):
        pl.semaphore_signal(know0, inc=1, device_id=dev(x, y, z + d, c), device_id_type=MESH)

    def arrived_y(k):
        for xs in range(NX):
            @pl.when((odd == 0) | (k > 0) | (xs != x))
            def _():
                gy(k, xs, 1 - odd).wait_recv()
                gc(origin(k, 1 - odd), xs, c).start()

    each(4, arrived_y)

    for copy in loads[2:]:
        copy.wait()

    for d in (4, -4):
        pl.semaphore_signal(know1, inc=1, device_id=dev(x, y, z + d, c), device_id_type=MESH)

    def product(k, acc):
        zs = origin(k % 4, lax.rem(odd + k // 4, 2))
        for xs in range(NX):
            gc(zs, xs, 1 - c).wait_recv()
        for xs in range(NX):
            cols = pl.ds(pl.multiple_of((xs * RUN + zs) * 256, 256), 256)
            w = wbuf[zs, xs].reshape(2 * QB, QB)
            acc += jnp.dot(tok[:, cols], w, preferred_element_type=jnp.float32)
        return acc

    pre = lax.fori_loop(0, RUN, product, jnp.zeros((TOK, QB), jnp.float32))
    sig = jax.nn.sigmoid(pre)
    act_out[...] = (pre * sig).astype(jnp.bfloat16)
    delta = og[...].astype(jnp.float32) * sig * (1.0 + pre * (1.0 - sig))
    dt[...] = delta.astype(jnp.bfloat16).T

    spot, half = zl % 4, zl // 4
    there_half = 4 - 4 * half

    def across(n, parity):
        return there_half + 2 * jnp.where(half == 0, 1 - n, n) + parity

    def beside(n):
        last = jnp.where(spot < 2, 1 - spot, 5 - spot)
        return zl - spot + jnp.where(n == 2, last, jnp.where(spot < 2, 3 - n, n))

    def place(k):
        far = across(k % 2, jnp.where(k < 2, 1 - zl % 2, zl % 2))
        return jnp.where(k < 4, far, jnp.where(k < 7, beside(k - 4), zl))

    def sib(k, side):
        return pltpu.make_async_remote_copy(
            src_ref=cod.at[k, side], dst_ref=sibin.at[k], send_sem=sib_s.at[k], recv_sem=sib_r.at[k],
            device_id=other, device_id_type=MESH,
        )

    def rx(k, d):
        return pltpu.make_async_remote_copy(
            src_ref=xout.at[k, mod(x + d, NX)], dst_ref=xin.at[k, d - 1], send_sem=rx_s.at[k, d - 1],
            recv_sem=rx_r.at[k, d - 1], device_id=along_x[d], device_id_type=MESH,
        )

    def rz(k):
        return pltpu.make_async_remote_copy(
            src_ref=zout.at[k], dst_ref=zin.at[zl], send_sem=rz_s.at[k], recv_sem=rz_r.at[zl],
            device_id=(group, block(x, place(k), c)), device_id_type=MESH,
        )

    def pair(k):
        return pltpu.make_async_remote_copy(
            src_ref=zout.at[k], dst_ref=zpair.at[k], send_sem=rz_s.at[k], recv_sem=pair_r.at[k],
            device_id=(group, block(x, zl + 1 - 2 * (zl % 2), c)), device_id_type=MESH,
        )

    def rz_wait(there):
        pltpu.make_async_remote_copy(
            src_ref=zout.at[0], dst_ref=zin.at[there], send_sem=rz_s.at[0], recv_sem=rz_r.at[there],
            device_id=other, device_id_type=MESH,
        ).wait_recv()

    def coded(k):
        zs = 7 - place(k)
        for xs in range(NX):
            cols = pl.ds(pl.multiple_of((xs * RUN + zs) * 256, 256), 256)
            part = jnp.dot(dt[...], tok[:, cols], preferred_element_type=jnp.float32)
            for cs in range(2):
                scaled = part[:, cs * QB:(cs + 1) * QB] * pow2(-gexp[block(xs, zs, cs)])
                cod[k, cs, xs] = jnp.clip(scaled, -code_limit, code_limit).astype(jnp.bfloat16)
        sib(k, 1 - c).start()

    def over_cores(k):
        sib(k, 1 - c).wait_recv()
        for xs in range(NX):
            both = cod[k, c, xs].astype(jnp.float32) + sibin[k, xs].astype(jnp.float32)
            xout[k, xs] = both.astype(jnp.bfloat16)
        for d in (2, 1, 3):
            rx(k, d).start()

    def over_x(k):
        total = xout[k, x].astype(jnp.float32)
        for d in (1, 3, 2):
            rx(k, d).wait_recv()
            total += xin[k, d - 1].astype(jnp.float32)

        @pl.when((k == 2) | (k == 3))
        def _():
            pair(k - 2).wait_recv()
            zout[k] = (total + zpair[k - 2].astype(jnp.float32)).astype(jnp.bfloat16)

        @pl.when((k < 2) | (k > 3))
        def _():
            zout[k] = total.astype(jnp.bfloat16)

        @pl.when(k < 2)
        def _():
            pair(k).start()

        @pl.when((k > 1) & (k < 7))
        def _():
            rz(k).start()

    def front(k):
        @pl.when(k < 8)
        def _():
            coded(k)

        @pl.when(k >= 4)
        def _():
            over_cores(k - 4)

    each(12, front)

    mirror = 7 - zl

    def piece(k):
        dy = jnp.where(k % 4 == 0, 2, jnp.where(k % 4 == 3, 0, 2 * (k % 4) - 1))
        side = jnp.where(zl < 4, 1, 3)
        dz = jnp.where(k // 4 == 0, 2, jnp.where(k // 4 == 1, side, jnp.where(k // 4 == 2, 0, 4 - side)))
        there = mod(y + dy, NY) * 4 + mod(z // RUN + dz, 4)
        return pltpu.make_async_remote_copy(
            src_ref=pout.at[there], dst_ref=pin.at[k], send_sem=p_s.at[k], recv_sem=p_r.at[k],
            device_id=(there, block(x, mirror, c)), device_id_type=MESH,
        )

    def over_run():
        def add_z(k, acc):
            there = jnp.where(k < 2, across(k, zl % 2), beside(k - 2))
            rz_wait(there)
            return acc + zin[there].astype(jnp.float32)

        first = lax.fori_loop(0, 5, add_z, zout[7].astype(jnp.float32))
        recoded = jnp.clip(first * pow2(-rexp[block(x, mirror, c)]), -code_limit, code_limit)
        recoded = recoded.astype(jnp.bfloat16).astype(jnp.float32)
        pout[...] = recoded.T.reshape(16, 8, QB)
        pl.semaphore_wait(know2, 2)
        for k in range(16):
            piece(k).start()

    def back(k):
        @pl.when(k == 0)
        def _():
            pl.semaphore_wait(know0, 2)

        @pl.when(k == 2)
        def _():
            pl.semaphore_wait(know1, 2)
            for d in (8, -8):
                pl.semaphore_signal(know2, inc=1, device_id=dev(x, y, z + d, c), device_id_type=MESH)

        over_x(k)

    each(8, back)
    over_run()

    @pl.when(odd == 0)
    def _():
        for copy in from_own + passed + [passed_far]:
            copy.wait_send()

    def sent4(k):
        for d in (1, 2, 3):
            gx(k, d, 0).wait_send()
        for xs in range(NX):
            @pl.when((odd == 1) | (k > 0) | (xs != x))
            def _():
                gy(k, xs, odd).wait_send()

    each(4, sent4)
    each(32, lambda k: gc(k // NX, k % NX, c).wait_send())

    def sent8(k):
        for d in (1, 2, 3):
            rx(k, d).wait_send()
        sib(k, 1 - c).wait_send()

    each(8, sent8)

    def sent_z(k):
        @pl.when(k < 2)
        def _():
            pair(k).wait_send()

        @pl.when(k > 1)
        def _():
            rz(k).wait_send()

    each(7, sent_z)
    each(16, lambda k: piece(k).wait_send())

    def add_piece(k, acc):
        piece(k).wait_recv()
        return acc + pin[k]

    summed = lax.fori_loop(0, 16, add_piece, jnp.zeros((8, QB), jnp.float32))
    mine = block(x, zl, c)
    grad_out[...] = summed * pow2(gexp[mine] + rexp[mine])


def body(tokens, weight_codes, weight_exp, grad_exp, recast_exp, out_grad):
    bf, f32 = jnp.bfloat16, jnp.float32
    dma, vmem = pltpu.SemaphoreType.DMA, pltpu.VMEM
    return pl.pallas_call(
        kernel,
        name="mlp_block",
        out_shape=(vmem((TOK, QB), bf), vmem((8, QB), f32)),
        in_specs=[pl.BlockSpec(memory_space=pltpu.HBM)] * 6,
        out_specs=(pl.BlockSpec(memory_space=pltpu.VMEM), pl.BlockSpec(memory_space=pltpu.VMEM)),
        scratch_shapes=[
            vmem((TOK, 8192), bf), vmem((QB, QB), bf), vmem((TOK, QB), bf),
            pltpu.SMEM((64,), jnp.int32), pltpu.SMEM((64,), jnp.int32), pltpu.SMEM((64,), jnp.int32),
            vmem((RUN, NX, 2, QB, QB), bf), vmem((QB, TOK), bf),
            vmem((RUN, 2, NX, QB, QB), bf), vmem((RUN, NX, QB, QB), bf),
            vmem((RUN, NX, QB, QB), bf), vmem((RUN, 3, QB, QB), bf),
            vmem((RUN, QB, QB), bf), vmem((RUN, QB, QB), bf), vmem((2, QB, QB), bf),
            vmem((16, 8, QB), f32), vmem((16, 8, QB), f32),
            dma((6,)),
            dma((7,)), dma((4,)), dma((4, 3)), dma((4, 3)), dma((4, 4)), dma((4, 4)), dma((8, 4)), dma((8, 4)),
            dma((8,)), dma((8,)), dma((8, 3)), dma((8, 3)), dma((8,)), dma((8,)), dma((2,)), dma((16,)), dma((16,)),
            pltpu.SemaphoreType.REGULAR, pltpu.SemaphoreType.REGULAR, pltpu.SemaphoreType.REGULAR,
        ],
        compiler_params=pltpu.CompilerParams(
            collective_id=0, has_side_effects=True, vmem_limit_bytes=60 * 2**20
        ),
    )(tokens, weight_codes, weight_exp, grad_exp, recast_exp, out_grad)


def solution(mesh):
    placed = (
        P(("group", "inner"), None),
        P("inner", None),
        P(),
        P(),
        P(),
        P(("group", "inner"), None),
    )
    return jax.shard_map(
        body,
        mesh=mesh,
        in_specs=placed,
        out_specs=(P(("group", "inner"), None), P(("inner", "group"), None)),
        check_vma=False,
    )
```
